256 devices in a mesh: ctx: 32 (over z_lo, y, x), vis: 8 (over z_hi, core).
Axes of the slice: x: 4, y: 4, z: 8 (z_hi: 4, z_lo: 2; z = z_hi * 2 + z_lo), core: 2. Of those that a mesh axis runs over, the one named last changes fastest.
Arguments:
- text_q: bfloat16 [8192, 8192], P('ctx', 'vis'), may hold values from -96 to 96
- text_k: bfloat16 [8192, 1024], P('ctx', 'vis'), may hold values from -4 to 4
- text_v: bfloat16 [8192, 1024], P('ctx', 'vis'), may hold values from -6 to 6
- cross_q: bfloat16 [8192, 8192], P('ctx', 'vis'), may hold values from -100 to 100
- vision_k: bfloat16 [8, 1024, 1024], P('vis', 'ctx'), may hold values from -100 to 100
- vision_v: bfloat16 [8, 1024, 1024], P('vis', 'ctx'), may hold values from -6 to 6
- q_gain: float32 [128], replicated, may hold values from 1 to 6.5
- k_gain: float32 [128], replicated, may hold values from 1 to 6.5
- head_gate: float32 [64], P('vis'), may hold values from 0.3 to 2
- adapter_down: bfloat16 [8192, 64], P('vis'), may hold values from -0.0625 to 0.0625
- image_ids: int32 [8192], P('ctx'), may hold values from -1 to 7, as said below
- image_slot: int32 [8], replicated, may hold values from 0 to 7, each once
Outputs:
- mixed_out: bfloat16 [8192, 8192], P('ctx', 'vis')
- lowrank: float32 [8192, 64], P('ctx')
The draws below stay inside these ranges and needn't reach their ends.
Inputs may be any that keep to these rules, and one draw needn't show every extreme that they name: `image_ids`: never falls along the text; -1 marks the tokens before the first image; the tokens of every aligned block of 256 read at most 2 images, which are consecutive, and every image is read by a run of more than 256 tokens. `image_slot`: each slot holds one image.
All inputs are finite; a program needn't handle non-finite values.
Results may differ from the reference program's by a relative error of at most 0.015.
The reference program's roundings to bfloat16 on the way count: a program that leaves them out, or rounds other values in their place, can miss the bound.
Values may be sent and summed in bfloat16 or wider, within the bound.
No kernel may reach another device: no remote copies, remote signals or barrier semaphores. Data moves between devices by JAX's collectives and lax.ppermute only.
A program may use at most 64 MiB of HBM per device.

```python
import math
import jax
import jax.numpy as jnp
from jax import lax

H = 64
KVH = 8
HD = 128
RANK = 64
TOK_DEV = 256
IMG_SPAN = 2
TEXT = 8192
VROWS = 1024
IMAGES = 8


def text_keys(key):
    return jnp.clip(jax.random.normal(jax.random.fold_in(key, 21), (TEXT, KVH * HD), jnp.float32), -4.0, 4.0)


def gain_pair(key, lowest, highest):
    gain_key = jax.random.fold_in(key, 51)
    query_key, vision_key = jax.random.split(gain_key)
    gain_q = jax.random.uniform(query_key, (HD,), jnp.float32, lowest, highest)
    gain_k = jax.random.uniform(vision_key, (HD,), jnp.float32, lowest, highest)
    return (gain_q, gain_k)


def draw_text_k(key, part):
    base_rows = text_keys(key)
    return base_rows.astype(jnp.bfloat16)


def draw_text_q(key, part):
    key = jax.random.fold_in(key, 5)
    queries = jnp.clip(jax.random.normal(key, (TEXT, H * HD), jnp.float32), -4.0, 4.0) * 2.5
    return queries.astype(jnp.bfloat16)


def draw_q_gain(key, part):
    gain_q, gain_k = gain_pair(key, 1.0, 2.2)
    return gain_q


def draw_k_gain(key, part):
    gain_q, gain_k = gain_pair(key, 1.0, 2.2)
    return gain_k


def draw_vision_k(key, part):
    key = jax.random.fold_in(key, 7)
    column_key, scale_key, value_key = jax.random.split(key, 3)
    column = jnp.exp(jax.random.uniform(column_key, (KVH, HD), jnp.float32, 0.0, math.log(10.0)))
    row_scale = jnp.exp(jax.random.uniform(scale_key, (IMAGES, VROWS, KVH, 1), jnp.float32, 0.0, math.log(10.0)))
    vision = jnp.clip(jax.random.normal(value_key, (IMAGES, VROWS, KVH, HD), jnp.float32), -4.0, 4.0) * row_scale * column
    return jnp.clip(vision, -100.0, 100.0).reshape(IMAGES, VROWS, KVH * HD).astype(jnp.bfloat16)


def draw_cross_q(key, part):
    key = jax.random.fold_in(key, 9)
    column_key, scale_key, value_key = jax.random.split(key, 3)
    column = jnp.exp(jax.random.uniform(column_key, (H, HD), jnp.float32, 0.0, math.log(10.0)))
    row_scale = jnp.exp(jax.random.uniform(scale_key, (TEXT, H, 1), jnp.float32, 0.0, math.log(10.0)))
    queries = jnp.clip(jax.random.normal(value_key, (TEXT, H, HD), jnp.float32), -4.0, 4.0) * row_scale * column
    return jnp.clip(queries, -100.0, 100.0).reshape(TEXT, H * HD).astype(jnp.bfloat16)


def draw_image_ids(key, part):
    key = jax.random.fold_in(key, 41)
    image_span = TEXT // IMAGES
    offsets = jax.random.randint(key, (IMAGES,), 1, TOK_DEV)
    starts = jnp.arange(IMAGES, dtype=jnp.int32) * image_span + offsets.astype(jnp.int32)
    positions = jnp.arange(TEXT, dtype=jnp.int32)
    return jnp.sum((positions[:, None] >= starts[None, :]).astype(jnp.int32), axis=1) - 1


def levels(key, dims, cuts, low, largest):
    factor_of, own = 1.0, jax.random.fold_in(key, 6)
    for dim, blocks in cuts:
        steps = jnp.exp(jax.random.uniform(jax.random.fold_in(own, dim), (blocks,), jnp.float32, low / len(cuts), largest / len(cuts)))
        factor_of = factor_of * jnp.repeat(steps, dims[dim] // blocks).reshape([-1 if axis == dim else 1 for axis in range(len(dims))])
    return factor_of


def scatter_about(stream_key, extent, scale, limit, cuts=(), kind=jnp.bfloat16):
    values = scale * jax.random.normal(stream_key, extent, jnp.float32)
    if cuts:
        values = values * levels(stream_key, extent, cuts, -0.22, 0.18)
    return jnp.clip(values, -limit, limit).astype(kind)


def setup_inputs(seed: int = 0) -> dict:
    streams_of = jax.random.split(jax.random.key(seed), 13)
    text_q = draw_text_q(jax.random.fold_in(streams_of[12], 71), 0)
    text_k = draw_text_k(jax.random.fold_in(streams_of[12], 71), 0)
    text_v = scatter_about(streams_of[2], (TEXT, KVH * HD), 1.0, 6.0, ((0, 32), (1, 8)))
    cross_q = draw_cross_q(jax.random.fold_in(streams_of[12], 71), 0)
    vision_k = draw_vision_k(jax.random.fold_in(streams_of[12], 71), 0)
    vision_v = scatter_about(streams_of[5], (IMAGES, VROWS, KVH * HD), 1.0, 6.0, ((0, 8), (1, 32)))
    q_gain = draw_q_gain(jax.random.fold_in(streams_of[12], 71), 0)
    k_gain = draw_k_gain(jax.random.fold_in(streams_of[12], 71), 0)
    head_gate = jnp.clip(0.3 + 1.7 * jax.random.uniform(streams_of[8], (H,), jnp.float32) ** levels(streams_of[8], (H,), ((0, 8),), -0.2, 0.2), 0.3, 2.0)
    adapter_down = scatter_about(streams_of[9], (H * HD, RANK), (H * HD) ** -0.5, 0.0625, ((0, 8),))
    image_ids = draw_image_ids(jax.random.fold_in(streams_of[12], 71), 0)
    image_slot = jax.random.permutation(streams_of[11], IMAGES).astype(jnp.int32)
    return {"text_q": text_q, "text_k": text_k, "text_v": text_v, "cross_q": cross_q, "vision_k": vision_k, "vision_v": vision_v, "q_gain": q_gain, "k_gain": k_gain, "head_gate": head_gate, "adapter_down": adapter_down, "image_ids": image_ids, "image_slot": image_slot}


EPSILON = 1e-05

def rms_scale(values, weights):
    widened = values.astype(jnp.float32)
    mean_sq = lax.optimization_barrier(jnp.mean(widened * widened, axis=-1, keepdims=True))
    return widened * lax.rsqrt(mean_sq + EPSILON) * weights

def softmax_parts(scores):
    highest = lax.optimization_barrier(jnp.max(scores, axis=-1, keepdims=True))
    powers = jnp.exp(scores - highest)
    totals = lax.optimization_barrier(jnp.sum(powers, axis=-1))
    narrow = lax.optimization_barrier(powers.astype(jnp.bfloat16)).astype(jnp.float32)
    return (narrow, totals)

def reference(text_q, text_k, text_v, cross_q, vision_k, vision_v, q_gain, k_gain, head_gate, adapter_down, image_ids, image_slot):
    group_size = H // KVH
    score_scale = 1.0 / math.sqrt(HD)
    block_rows = math.gcd(TOK_DEV, 64)
    block_count = TEXT // block_rows
    key_rows = text_k.astype(jnp.float32).reshape(TEXT, KVH, HD)
    value_rows = text_v.astype(jnp.float32).reshape(TEXT, KVH, HD)
    positions = jnp.arange(TEXT, dtype=jnp.int32)
    query_all = text_q.reshape(TEXT, KVH, group_size, HD)
    cross_normed = rms_scale(cross_q.reshape(TEXT, H, HD), q_gain).astype(jnp.bfloat16).reshape(TEXT, KVH, group_size, HD)
    vision_normed = rms_scale(vision_k.reshape(IMAGES, VROWS, KVH, HD), k_gain).astype(jnp.bfloat16)
    vision_values = vision_v.reshape(IMAGES, VROWS, KVH, HD)

    def self_block(block_index):
        row_start = (block_index * block_rows).astype(jnp.int32)
        queries = lax.dynamic_slice_in_dim(query_all, row_start, block_rows, 0).astype(jnp.float32)
        query_pos = row_start + jnp.arange(block_rows, dtype=jnp.int32)
        scores = jnp.einsum('tkgd,skd->tkgs', queries, key_rows) * score_scale
        allowed = (positions[None, :] <= query_pos[:, None])[:, None, None, :]
        scores = jnp.where(allowed, scores, -jnp.inf)
        narrow, totals = softmax_parts(scores)
        return jnp.einsum('tkgs,skd->tkgd', narrow, value_rows) / totals[..., None]

    def cross_block(block_index):
        row_start = (block_index * block_rows).astype(jnp.int32)
        token_images = lax.dynamic_slice_in_dim(image_ids, row_start, block_rows, 0)
        first_image = jnp.maximum(token_images[0], 0)
        queries = lax.dynamic_slice_in_dim(cross_normed, row_start, block_rows, 0).astype(jnp.float32)
        result = jnp.zeros((block_rows, KVH, group_size, HD), jnp.float32)
        for offset in range(IMG_SPAN):
            image_index = first_image + offset
            slot_index = image_slot[jnp.minimum(image_index, IMAGES - 1)].astype(jnp.int32)
            image_keys = lax.dynamic_index_in_dim(vision_normed, slot_index, 0, keepdims=False).astype(jnp.float32)
            image_values = lax.dynamic_index_in_dim(vision_values, slot_index, 0, keepdims=False).astype(jnp.float32)
            scores = jnp.einsum('tkgd,skd->tkgs', queries, image_keys) * score_scale
            narrow, totals = softmax_parts(scores)
            attended = jnp.einsum('tkgs,skd->tkgd', narrow, image_values) / totals[..., None]
            result = jnp.where((token_images == image_index)[:, None, None, None], attended, result)
        return result
    indices = jnp.arange(block_count, dtype=jnp.int32)
    self_att = lax.map(self_block, indices).reshape(TEXT, H, HD)
    cross_att = lax.map(cross_block, indices).reshape(TEXT, H, HD)
    gate_values = jnp.tanh(head_gate)
    mixed_out = (self_att + gate_values[None, :, None] * cross_att).astype(jnp.bfloat16).reshape(TEXT, H * HD)
    lowrank = jnp.dot(mixed_out, adapter_down, preferred_element_type=jnp.float32)
    return (mixed_out, lowrank)
```

```python
import functools
import math

import jax
import jax.numpy as jnp
from jax import lax
from jax.experimental import pallas as pl
from jax.experimental.pallas import tpu as pltpu
from jax.sharding import PartitionSpec as P

HD = 128
EPSILON = 1e-05
MASKED = -1e30
SCALE = HD**-0.5 / math.log(2.0)
CHUNK = 4
ID_ROWS = 16

VMEM = pl.BlockSpec(memory_space=pltpu.VMEM)
SMEM = pl.BlockSpec(memory_space=pltpu.SMEM)


def rows_dot(left, right):
    return lax.dot_general(left, right, (((1,), (1,)), ((), ())), preferred_element_type=jnp.float32)


def dot(left, right):
    return jnp.dot(left, right, preferred_element_type=jnp.float32)


def rms_scale(values, weights):
    widened = values.astype(jnp.float32)
    mean_sq = jnp.mean(widened * widened, axis=-1, keepdims=True)
    return widened * lax.rsqrt(mean_sq + EPSILON) * weights


def split_scaled(queries):
    scaled = queries.astype(jnp.float32) * SCALE
    high = scaled.astype(jnp.bfloat16)
    low = (scaled - high.astype(jnp.float32)).astype(jnp.bfloat16)
    return jnp.concatenate([high, low], axis=1)


def tile_lanes(rows, width):
    return jnp.concatenate([rows] * (width // HD), axis=1)


def row_peak(scores):
    peak = scores[:, :HD]
    for start in range(HD, scores.shape[1], HD):
        peak = jnp.maximum(peak, scores[:, start : start + HD])
    return jnp.broadcast_to(jnp.max(peak, axis=1, keepdims=True), peak.shape)


def head_columns(head):
    return slice(head * HD, (head + 1) * HD)


def pipelined(heads, scores_of, use):
    scores = scores_of(0)
    for head in range(heads):
        following = scores_of(head + 1) if head + 1 < heads else None
        use(head, scores)
        scores = following


def vision_kernel(keys_ref, values_ref, gain_ref, out_ref):
    for group in range(out_ref.shape[0]):
        columns = head_columns(group)
        out_ref[group, :, :HD] = rms_scale(keys_ref[:, columns], gain_ref[...]).astype(jnp.bfloat16)
        out_ref[group, :, HD:] = values_ref[:, columns]


def select_kernel(slots_ref, rows_ref, out_ref):
    def copy(index, carry):
        out_ref[index] = rows_ref[slots_ref[index]]
        return carry

    lax.fori_loop(0, out_ref.shape[0], copy, 0, unroll=8)


def self_kernel(index_ref, q_ref, kv_ref, out_ref, queries, peaks, totals, sums):
    rows = q_ref.shape[0]
    heads = q_ref.shape[1] // HD
    index = index_ref[0]
    full_chunks = index // CHUNK
    width = CHUNK * rows
    for head in range(heads):
        queries[head] = split_scaled(q_ref[:, head_columns(head)])

    def load(chunk):
        blocks = pl.ds(chunk * CHUNK, CHUNK)
        keys = kv_ref[blocks, :rows, :HD].reshape(width, HD)
        values = kv_ref[blocks, :rows, HD:].reshape(width, HD)
        return (
            jnp.concatenate([keys, keys], axis=1),
            jnp.concatenate([values, jnp.ones_like(values)], axis=1),
        )

    last_keys, last_values = load(full_chunks)
    query_row = lax.broadcasted_iota(jnp.int32, (rows, width), 0) + (index - full_chunks * CHUNK) * rows
    allowed = lax.broadcasted_iota(jnp.int32, (rows, width), 1) <= query_row

    def first_scores(head):
        return jnp.where(allowed, rows_dot(queries[head], last_keys), MASKED)

    def first_use(head, scores):
        peak = row_peak(scores)
        powers = jnp.exp2(scores - tile_lanes(peak, width)).astype(jnp.bfloat16)
        mixed = dot(powers, last_values)
        peaks[head] = peak
        sums[head] = mixed[:, :HD]
        totals[head] = mixed[:, HD:]

    pipelined(heads, first_scores, first_use)

    def step(chunk, carry):
        keys, values = load(chunk)

        def scores_of(head):
            return rows_dot(queries[head], keys)

        def use(head, scores):
            old_peak = peaks[head]
            peak = jnp.maximum(old_peak, row_peak(scores))
            powers = jnp.exp2(scores - tile_lanes(peak, width)).astype(jnp.bfloat16)
            factor = jnp.exp2(old_peak - peak)
            mixed = dot(powers, values)
            peaks[head] = peak
            sums[head] = sums[head] * factor + mixed[:, :HD]
            totals[head] = totals[head] * factor + mixed[:, HD:]

        pipelined(heads, scores_of, use)
        return carry

    lax.fori_loop(0, full_chunks, step, 0)
    for head in range(heads):
        out_ref[:, head_columns(head)] = sums[head] / totals[head]


def cross_kernel(
    needed_ref, q_ref, gain_ref, gate_ref, ids_ref, kv_ref, self_ref, down_ref, out_ref, rank_ref, queries, crossed
):
    rows = q_ref.shape[0]
    heads = q_ref.shape[1] // HD
    sources, _, part, _ = kv_ref.shape
    width = sources * part
    crossed[...] = jnp.zeros_like(crossed)
    gates = jnp.tanh(gate_ref[...])

    @pl.when(needed_ref[0] + needed_ref[1] > 0)
    def _():
        for head in range(heads):
            normed = rms_scale(q_ref[:, head_columns(head)], gain_ref[...]).astype(jnp.bfloat16)
            queries[head] = split_scaled(normed)

    def attend(offset):
        keys = kv_ref[:, offset, :, :HD].reshape(width, HD)
        values = kv_ref[:, offset, :, HD:].reshape(width, HD)
        keys = jnp.concatenate([keys, keys], axis=1)
        values = jnp.concatenate([values, jnp.ones_like(values)], axis=1)
        matches = jnp.broadcast_to(ids_ref[...], (rows, HD)) == needed_ref[2] + offset

        def scores_of(head):
            return rows_dot(queries[head], keys)

        def use(head, scores):
            powers = jnp.exp2(scores - tile_lanes(row_peak(scores), width)).astype(jnp.bfloat16)
            mixed = dot(powers, values)
            attended = mixed[:, :HD] / mixed[:, HD:]
            crossed[head] = jnp.where(matches, attended, crossed[head])

        pipelined(heads, scores_of, use)

    for offset in range(2):
        pl.when(needed_ref[offset] > 0)(functools.partial(attend, offset))

    for head in range(heads):
        gate = gates[head : head + 1]
        out_ref[:, head_columns(head)] = (self_ref[:, head_columns(head)] + gate * crossed[head]).astype(jnp.bfloat16)
    rank = dot(out_ref[...], down_ref[...]).astype(jnp.bfloat16)
    rank_ref[...] = jnp.concatenate([rank[: rows // 2], rank[rows // 2 :]], axis=1)


def local(
    text_q,
    text_k,
    text_v,
    cross_q,
    vision_k,
    vision_v,
    q_gain,
    k_gain,
    head_gate,
    adapter_down,
    image_ids,
    image_slot,
):
    rows, q_width = text_q.shape
    heads = q_width // HD
    ctx = lax.axis_size("ctx")
    vis = lax.axis_size("vis")
    part = vision_k.shape[1]
    images = image_slot.shape[0]
    params = pltpu.CompilerParams(vmem_limit_bytes=48 * 2**20)
    index = lax.axis_index("ctx").astype(jnp.int32)
    shape = jax.ShapeDtypeStruct

    first = jnp.maximum(image_ids[0], 0)
    id_rows = jnp.broadcast_to(first.astype(jnp.bfloat16), (ID_ROWS, 2 * HD))
    payload = jnp.concatenate([jnp.concatenate([text_k, text_v], axis=1), id_rows], axis=0)
    text_kv = lax.all_to_all(jnp.broadcast_to(payload[None], (ctx,) + payload.shape), "ctx", 0, 0)

    groups = pl.pallas_call(
        vision_kernel,
        out_shape=shape((vis, part, 2 * HD), jnp.bfloat16),
        in_specs=[VMEM] * 3,
        out_specs=VMEM,
    )(vision_k[0], vision_v[0], k_gain.reshape(1, HD))
    slots_kv = lax.all_to_all(groups, "vis", 0, 0)

    firsts = text_kv[:, rows, 0].astype(jnp.int32)
    pairs = jnp.stack([firsts, jnp.minimum(firsts + 1, images - 1)], axis=1).reshape(-1)
    chosen = jnp.sum(jnp.where(pairs[:, None] == jnp.arange(images)[None, :], image_slot[None, :], 0), axis=1)
    picked = pl.pallas_call(
        select_kernel,
        out_shape=shape((2 * ctx, part, 2 * HD), jnp.bfloat16),
        in_specs=[SMEM, VMEM],
        out_specs=VMEM,
    )(chosen.astype(jnp.int32), slots_kv)
    image_kv = lax.all_to_all(picked.reshape(ctx, 2, part, 2 * HD), "ctx", 0, 0)

    state = pltpu.VMEM((heads, rows, HD), jnp.float32)
    self_att = pl.pallas_call(
        self_kernel,
        out_shape=shape((rows, q_width), jnp.float32),
        in_specs=[SMEM, VMEM, VMEM],
        out_specs=VMEM,
        scratch_shapes=[pltpu.VMEM((heads, rows, 2 * HD), jnp.bfloat16), state, state, state],
        compiler_params=params,
        cost_estimate=pl.CostEstimate(flops=17 * 10**9, bytes_accessed=6 * 10**6, transcendentals=17 * 10**6),
    )(index.reshape(1), text_q, text_kv)

    needed = jnp.stack([jnp.any(image_ids == first), jnp.any(image_ids == first + 1), first]).astype(jnp.int32)
    mixed_out, partial = pl.pallas_call(
        cross_kernel,
        out_shape=(shape((rows, q_width), jnp.bfloat16), shape((rows // 2, 2 * adapter_down.shape[1]), jnp.bfloat16)),
        in_specs=[SMEM] + [VMEM] * 7,
        out_specs=(VMEM, VMEM),
        scratch_shapes=[pltpu.VMEM((heads, rows, 2 * HD), jnp.bfloat16), state],
        compiler_params=params,
        cost_estimate=pl.CostEstimate(flops=4 * 10**9, bytes_accessed=4 * 10**6, transcendentals=4 * 10**6),
    )(
        needed,
        cross_q,
        q_gain.reshape(1, HD),
        jnp.broadcast_to(head_gate[:, None], (heads, HD)),
        image_ids[:, None],
        image_kv,
        self_att,
        adapter_down,
    )
    partials = lax.all_to_all(jnp.broadcast_to(partial[None], (vis,) + partial.shape), "vis", 0, 0)
    summed = jnp.sum(partials.astype(jnp.float32), axis=0)
    rank = adapter_down.shape[1]
    lowrank = jnp.concatenate([summed[:, :rank], summed[:, rank:]], axis=0)
    return (mixed_out, lowrank)


def solution(mesh):
    return jax.shard_map(
        local,
        mesh=mesh,
        in_specs=(
            P("ctx", "vis"),
            P("ctx", "vis"),
            P("ctx", "vis"),
            P("ctx", "vis"),
            P("vis", "ctx", None),
            P("vis", "ctx", None),
            P(),
            P(),
            P("vis"),
            P("vis", None),
            P("ctx"),
            P(),
        ),
        out_specs=(P("ctx", "vis"), P("ctx", None)),
        check_vma=False,
    )
```

```python
import functools
import math

import jax
import jax.numpy as jnp
from jax import lax
from jax.experimental import pallas as pl
from jax.experimental.pallas import tpu as pltpu
from jax.sharding import PartitionSpec as P

HD = 128
EPSILON = 1e-05
MASKED = -1e30
SCALE = HD**-0.5 / math.log(2.0)
CHUNK = 4
ID_ROWS = 16

VMEM = pl.BlockSpec(memory_space=pltpu.VMEM)
SMEM = pl.BlockSpec(memory_space=pltpu.SMEM)


def rows_dot(left, right):
    return lax.dot_general(left, right, (((1,), (1,)), ((), ())), preferred_element_type=jnp.float32)


def dot(left, right):
    return jnp.dot(left, right, preferred_element_type=jnp.float32)


def rms_scale(values, weights):
    widened = values.astype(jnp.float32)
    mean_sq = jnp.mean(widened * widened, axis=-1, keepdims=True)
    return widened * lax.rsqrt(mean_sq + EPSILON) * weights


def split_scaled(queries):
    scaled = queries.astype(jnp.float32) * SCALE
    high = scaled.astype(jnp.bfloat16)
    low = (scaled - high.astype(jnp.float32)).astype(jnp.bfloat16)
    return jnp.concatenate([high, low], axis=1)


def tile_lanes(rows, width):
    return jnp.concatenate([rows] * (width // HD), axis=1)


def row_peak(scores):
    peak = scores[:, :HD]
    for start in range(HD, scores.shape[1], HD):
        peak = jnp.maximum(peak, scores[:, start : start + HD])
    return jnp.broadcast_to(jnp.max(peak, axis=1, keepdims=True), peak.shape)


def head_columns(head):
    return slice(head * HD, (head + 1) * HD)


def pipelined(heads, scores_of, use):
    scores = scores_of(0)
    for head in range(heads):
        following = scores_of(head + 1) if head + 1 < heads else None
        use(head, scores)
        scores = following


def payload_kernel(ids_ref, keys_ref, values_ref, out_ref):
    rows = keys_ref.shape[0]
    out_ref[:rows, :HD] = keys_ref[...]
    out_ref[:rows, HD:] = values_ref[...]
    first = jnp.maximum(ids_ref[0], 0).astype(jnp.float32)
    out_ref[rows:] = jnp.broadcast_to(first, (ID_ROWS, 2 * HD)).astype(jnp.bfloat16)


def slots_kernel(place_ref, own_ref, other_ref, out_ref):
    rows = own_ref.shape[0] - ID_ROWS
    late = place_ref[0] == 1
    index = place_ref[1]

    def fill(slot, carry):
        wanted = jnp.logical_and(late, index > slot)

        @pl.when(wanted)
        def _():
            out_ref[slot, :rows] = other_ref[:rows]

        @pl.when(jnp.logical_not(wanted))
        def _():
            out_ref[slot, :rows] = own_ref[:rows]

        out_ref[slot, rows:, :HD] = own_ref[rows:, :HD]
        out_ref[slot, rows:, HD:] = other_ref[rows:, HD:]
        return carry

    lax.fori_loop(0, out_ref.shape[0], fill, 0)


def vision_kernel(keys_ref, values_ref, gain_ref, out_ref):
    for group in range(out_ref.shape[0]):
        columns = head_columns(group)
        out_ref[group, :, :HD] = rms_scale(keys_ref[:, columns], gain_ref[...]).astype(jnp.bfloat16)
        out_ref[group, :, HD:] = values_ref[:, columns]


def select_kernel(slots_ref, rows_ref, out_ref):
    def copy(index, carry):
        out_ref[index] = rows_ref[slots_ref[index]]
        return carry

    lax.fori_loop(0, out_ref.shape[0], copy, 0, unroll=8)


def attend_text(q_ref, kv_ref, masked_chunk, other_chunks, allowed_of, queries, peaks, totals, sums):
    rows = q_ref.shape[0]
    heads = q_ref.shape[1] // HD
    width = CHUNK * rows
    for head in range(heads):
        queries[head] = split_scaled(q_ref[:, head_columns(head)])

    def load(chunk):
        blocks = pl.ds(chunk * CHUNK, CHUNK)
        keys = kv_ref[blocks, :rows, :HD].reshape(width, HD)
        values = kv_ref[blocks, :rows, HD:].reshape(width, HD)
        return (
            jnp.concatenate([keys, keys], axis=1),
            jnp.concatenate([values, jnp.ones_like(values)], axis=1),
        )

    masked_keys, masked_values = load(masked_chunk)
    row_index = lax.broadcasted_iota(jnp.int32, (rows, width), 0)
    column = lax.broadcasted_iota(jnp.int32, (rows, width), 1) + masked_chunk * width
    allowed = allowed_of(row_index, column)

    def first_scores(head):
        return jnp.where(allowed, rows_dot(queries[head], masked_keys), MASKED)

    def first_use(head, scores):
        peak = row_peak(scores)
        powers = jnp.exp2(scores - tile_lanes(peak, width)).astype(jnp.bfloat16)
        mixed = dot(powers, masked_values)
        peaks[head] = peak
        sums[head] = mixed[:, :HD]
        totals[head] = mixed[:, HD:]

    pipelined(heads, first_scores, first_use)

    def step(turn, carry):
        keys, values = load(turn + (turn >= masked_chunk).astype(jnp.int32))

        def scores_of(head):
            return rows_dot(queries[head], keys)

        def use(head, scores):
            old_peak = peaks[head]
            peak = jnp.maximum(old_peak, row_peak(scores))
            powers = jnp.exp2(scores - tile_lanes(peak, width)).astype(jnp.bfloat16)
            factor = jnp.exp2(old_peak - peak)
            mixed = dot(powers, values)
            peaks[head] = peak
            sums[head] = sums[head] * factor + mixed[:, :HD]
            totals[head] = totals[head] * factor + mixed[:, HD:]

        pipelined(heads, scores_of, use)
        return carry

    lax.fori_loop(0, other_chunks, step, 0)


def first_kernel(place_ref, own_q_ref, sent_q_ref, kv_ref, out_ref, logs_ref, ship_ref, queries, peaks, totals, sums):
    rows = own_q_ref.shape[0]
    heads = own_q_ref.shape[1] // HD
    slots = kv_ref.shape[0]
    late = place_ref[0] == 1
    index = place_ref[1]
    state = (queries, peaks, totals, sums)

    @pl.when(late)
    def _():
        def allowed(row, column):
            return jnp.logical_or(column <= row + index * rows, column >= (index + 1) * rows)

        attend_text(own_q_ref, kv_ref, index // CHUNK, slots // CHUNK - 1, allowed, *state)
        for head in range(heads):
            out_ref[:, head_columns(head)] = sums[head] / totals[head]
            logs_ref[head] = peaks[head] + jnp.log2(totals[head])

    @pl.when(jnp.logical_not(late))
    def _():
        count = slots - index

        def allowed(row, column):
            return column < count * rows

        attend_text(sent_q_ref, kv_ref, (count - 1) // CHUNK, (count - 1) // CHUNK, allowed, *state)
        lane = lax.broadcasted_iota(jnp.int32, (rows, HD), 1)
        coded = jnp.zeros((rows, HD), jnp.float32)
        for head in range(heads):
            ship_ref[:, head_columns(head)] = (sums[head] / totals[head]).astype(jnp.bfloat16)
            rest = peaks[head] + jnp.log2(totals[head])
            for term in range(3):
                rounded = rest.astype(jnp.bfloat16).astype(jnp.float32)
                coded = jnp.where(lane == term * heads + head, rounded, coded)
                rest = rest - rounded
        ship_ref[:, heads * HD :] = coded.astype(jnp.bfloat16)


def second_kernel(place_ref, q_ref, kv_ref, out_ref, queries, peaks, totals, sums):
    rows = q_ref.shape[0]
    index = place_ref[1]

    @pl.when(place_ref[0] == 0)
    def _():
        def allowed(row, column):
            return column <= row + index * rows

        attend_text(q_ref, kv_ref, index // CHUNK, index // CHUNK, allowed, queries, peaks, totals, sums)
        for head in range(q_ref.shape[1] // HD):
            out_ref[:, head_columns(head)] = sums[head] / totals[head]


def cross_kernel(
    place_ref,
    needed_ref,
    q_ref,
    gain_ref,
    gate_ref,
    ids_ref,
    kv_ref,
    early_ref,
    late_ref,
    logs_ref,
    sent_ref,
    down_ref,
    out_ref,
    rank_ref,
    queries,
    crossed,
):
    rows = q_ref.shape[0]
    heads = q_ref.shape[1] // HD
    sources, _, part, _ = kv_ref.shape
    width = sources * part
    crossed[...] = jnp.zeros_like(crossed)
    gates = jnp.tanh(gate_ref[...])

    @pl.when(needed_ref[0] + needed_ref[1] > 0)
    def _():
        for head in range(heads):
            normed = rms_scale(q_ref[:, head_columns(head)], gain_ref[...]).astype(jnp.bfloat16)
            queries[head] = split_scaled(normed)

    def attend(offset):
        keys = kv_ref[:, offset, :, :HD].reshape(width, HD)
        values = kv_ref[:, offset, :, HD:].reshape(width, HD)
        keys = jnp.concatenate([keys, keys], axis=1)
        values = jnp.concatenate([values, jnp.ones_like(values)], axis=1)
        matches = jnp.broadcast_to(ids_ref[...], (rows, HD)) == needed_ref[2] + offset

        def scores_of(head):
            return rows_dot(queries[head], keys)

        def use(head, scores):
            powers = jnp.exp2(scores - tile_lanes(row_peak(scores), width)).astype(jnp.bfloat16)
            mixed = dot(powers, values)
            attended = mixed[:, :HD] / mixed[:, HD:]
            crossed[head] = jnp.where(matches, attended, crossed[head])

        pipelined(heads, scores_of, use)

    for offset in range(2):
        pl.when(needed_ref[offset] > 0)(functools.partial(attend, offset))

    @pl.when(place_ref[0] == 0)
    def _():
        for head in range(heads):
            columns = head_columns(head)
            gate = gates[head : head + 1]
            out_ref[:, columns] = (early_ref[:, columns] + gate * crossed[head]).astype(jnp.bfloat16)

    @pl.when(place_ref[0] == 1)
    def _():
        coded = sent_ref[:, heads * HD :].astype(jnp.float32)
        for head in range(heads):
            columns = head_columns(head)
            sent_log = jnp.zeros((rows, 1), jnp.float32)
            for term in range(3):
                lane = term * heads + head
                sent_log = sent_log + coded[:, lane : lane + 1]
            own_log = logs_ref[head]
            sent_log = jnp.broadcast_to(sent_log, own_log.shape)
            peak = jnp.maximum(own_log, sent_log)
            own_part = jnp.exp2(own_log - peak)
            sent_part = jnp.exp2(sent_log - peak)
            mixed = own_part * late_ref[:, columns] + sent_part * sent_ref[:, columns].astype(jnp.float32)
            gate = gates[head : head + 1]
            out_ref[:, columns] = (mixed / (own_part + sent_part) + gate * crossed[head]).astype(jnp.bfloat16)

    rank = dot(out_ref[...], down_ref[...]).astype(jnp.bfloat16)
    rank_ref[...] = jnp.concatenate([rank[: rows // 2], rank[rows // 2 :]], axis=1)


def local(
    text_q,
    text_k,
    text_v,
    cross_q,
    vision_k,
    vision_v,
    q_gain,
    k_gain,
    head_gate,
    adapter_down,
    image_ids,
    image_slot,
):
    rows, q_width = text_q.shape
    heads = q_width // HD
    ctx = lax.axis_size("ctx")
    vis = lax.axis_size("vis")
    half = ctx // 2
    part = vision_k.shape[1]
    images = image_slot.shape[0]
    params = pltpu.CompilerParams(vmem_limit_bytes=40 * 2**20)
    index = lax.axis_index("ctx").astype(jnp.int32)
    place = jnp.stack([index // half, index % half])
    shape = jax.ShapeDtypeStruct

    payload = pl.pallas_call(
        payload_kernel,
        out_shape=shape((rows + ID_ROWS, 2 * HD), jnp.bfloat16),
        in_specs=[SMEM, VMEM, VMEM],
        out_specs=VMEM,
    )(image_ids, text_k, text_v)
    other = lax.ppermute(payload, "ctx", [(c, (c + half) % ctx) for c in range(ctx)])
    sent_q = lax.ppermute(text_q, "ctx", [(c, ctx - 1 - c) for c in range(half, ctx)])
    outgoing = pl.pallas_call(
        slots_kernel,
        out_shape=shape((half,) + payload.shape, jnp.bfloat16),
        in_specs=[SMEM, VMEM, VMEM],
        out_specs=VMEM,
    )(place, payload, other)
    planes = [list(range(half)), list(range(half, ctx))]
    text_kv = lax.all_to_all(outgoing, "ctx", 0, 0, axis_index_groups=planes)

    groups = pl.pallas_call(
        vision_kernel,
        out_shape=shape((vis, part, 2 * HD), jnp.bfloat16),
        in_specs=[VMEM] * 3,
        out_specs=VMEM,
    )(vision_k[0], vision_v[0], k_gain.reshape(1, HD))
    slots_kv = lax.all_to_all(groups, "vis", 0, 0)

    same = text_kv[:, rows, 0]
    across = text_kv[:, rows, HD]
    late = index >= half
    firsts = jnp.concatenate([jnp.where(late, across, same), jnp.where(late, same, across)]).astype(jnp.int32)
    pairs = jnp.stack([firsts, jnp.minimum(firsts + 1, images - 1)], axis=1).reshape(-1)
    chosen = jnp.sum(jnp.where(pairs[:, None] == jnp.arange(images)[None, :], image_slot[None, :], 0), axis=1)
    picked = pl.pallas_call(
        select_kernel,
        out_shape=shape((2 * ctx, part, 2 * HD), jnp.bfloat16),
        in_specs=[SMEM, VMEM],
        out_specs=VMEM,
    )(chosen.astype(jnp.int32), slots_kv)
    image_kv = lax.all_to_all(picked.reshape(ctx, 2, part, 2 * HD), "ctx", 0, 0)

    state = pltpu.VMEM((heads, rows, HD), jnp.float32)
    text_scratch = [pltpu.VMEM((heads, rows, 2 * HD), jnp.bfloat16), state, state, state]
    late_att, late_logs, ship = pl.pallas_call(
        first_kernel,
        out_shape=(
            shape((rows, q_width), jnp.float32),
            shape((heads, rows, HD), jnp.float32),
            shape((rows, q_width + HD), jnp.bfloat16),
        ),
        in_specs=[SMEM] + [VMEM] * 3,
        out_specs=(VMEM, VMEM, VMEM),
        scratch_shapes=text_scratch,
        compiler_params=params,
        cost_estimate=pl.CostEstimate(flops=9 * 10**9, bytes_accessed=6 * 10**6, transcendentals=9 * 10**6),
    )(place, text_q, sent_q, text_kv)
    sent = lax.ppermute(ship, "ctx", [(c, ctx - 1 - c) for c in range(half)])
    early_att = pl.pallas_call(
        second_kernel,
        out_shape=shape((rows, q_width), jnp.float32),
        in_specs=[SMEM] + [VMEM] * 2,
        out_specs=VMEM,
        scratch_shapes=text_scratch,
        compiler_params=params,
        cost_estimate=pl.CostEstimate(flops=9 * 10**9, bytes_accessed=6 * 10**6, transcendentals=9 * 10**6),
    )(place, text_q, text_kv)

    first = jnp.maximum(image_ids[0], 0)
    needed = jnp.stack([jnp.any(image_ids == first), jnp.any(image_ids == first + 1), first]).astype(jnp.int32)
    mixed_out, partial = pl.pallas_call(
        cross_kernel,
        out_shape=(shape((rows, q_width), jnp.bfloat16), shape((rows // 2, 2 * adapter_down.shape[1]), jnp.bfloat16)),
        in_specs=[SMEM] * 2 + [VMEM] * 10,
        out_specs=(VMEM, VMEM),
        scratch_shapes=[pltpu.VMEM((heads, rows, 2 * HD), jnp.bfloat16), state],
        compiler_params=params,
        cost_estimate=pl.CostEstimate(flops=4 * 10**9, bytes_accessed=4 * 10**6, transcendentals=4 * 10**6),
    )(
        place,
        needed,
        cross_q,
        q_gain.reshape(1, HD),
        jnp.broadcast_to(head_gate[:, None], (heads, HD)),
        image_ids[:, None],
        image_kv,
        early_att,
        late_att,
        late_logs,
        sent,
        adapter_down,
    )
    partials = lax.all_to_all(jnp.broadcast_to(partial[None], (vis,) + partial.shape), "vis", 0, 0)
    summed = jnp.sum(partials.astype(jnp.float32), axis=0)
    rank = adapter_down.shape[1]
    lowrank = jnp.concatenate([summed[:, :rank], summed[:, rank:]], axis=0)
    return (mixed_out, lowrank)


def solution(mesh):
    return jax.shard_map(
        local,
        mesh=mesh,
        in_specs=(
            P("ctx", "vis"),
            P("ctx", "vis"),
            P("ctx", "vis"),
            P("ctx", "vis"),
            P("vis", "ctx", None),
            P("vis", "ctx", None),
            P(),
            P(),
            P("vis"),
            P("vis", None),
            P("ctx"),
            P(),
        ),
        out_specs=(P("ctx", "vis"), P("ctx", None)),
        check_vma=False,
    )
```

```python
import functools
import math

import jax
import jax.numpy as jnp
from jax import lax
from jax.experimental import pallas as pl
from jax.experimental.pallas import tpu as pltpu
from jax.sharding import PartitionSpec as P

HD = 128
EPSILON = 1e-05
MASKED = -1e30
SCALE = HD**-0.5 / math.log(2.0)
CHUNK = 4
ID_ROWS = 16

VMEM = pl.BlockSpec(memory_space=pltpu.VMEM)
HBM = pl.BlockSpec(memory_space=pltpu.HBM)
SMEM = pl.BlockSpec(memory_space=pltpu.SMEM)


def rows_dot(left, right):
    return lax.dot_general(left, right, (((1,), (1,)), ((), ())), preferred_element_type=jnp.float32)


def dot(left, right):
    return jnp.dot(left, right, preferred_element_type=jnp.float32)


def rms_scale(values, weights):
    widened = values.astype(jnp.float32)
    mean_sq = jnp.mean(widened * widened, axis=-1, keepdims=True)
    return widened * lax.rsqrt(mean_sq + EPSILON) * weights


def split_scaled(queries):
    scaled = queries.astype(jnp.float32) * SCALE
    high = scaled.astype(jnp.bfloat16)
    low = (scaled - high.astype(jnp.float32)).astype(jnp.bfloat16)
    return jnp.concatenate([high, low], axis=1)


def tile_lanes(rows, width):
    return jnp.concatenate([rows] * (width // HD), axis=1)


def row_peak(scores):
    peak = scores[:, :HD]
    for start in range(HD, scores.shape[1], HD):
        peak = jnp.maximum(peak, scores[:, start : start + HD])
    return jnp.broadcast_to(jnp.max(peak, axis=1, keepdims=True), peak.shape)


def head_columns(head):
    return slice(head * HD, (head + 1) * HD)


def pipelined(heads, scores_of, use):
    scores = scores_of(0)
    for head in range(heads):
        following = scores_of(head + 1) if head + 1 < heads else None
        use(head, scores)
        scores = following


def payload_kernel(ids_ref, keys_ref, values_ref, out_ref, key_sem, value_sem):
    rows = keys_ref.shape[0]
    key_copy = pltpu.make_async_copy(keys_ref, out_ref.at[pl.ds(0, rows), pl.ds(0, HD)], key_sem)
    value_copy = pltpu.make_async_copy(values_ref, out_ref.at[pl.ds(0, rows), pl.ds(HD, HD)], value_sem)
    key_copy.start()
    value_copy.start()
    first = jnp.maximum(ids_ref[0], 0).astype(jnp.float32)
    out_ref[rows:] = jnp.broadcast_to(first, (ID_ROWS, 2 * HD)).astype(jnp.bfloat16)
    key_copy.wait()
    value_copy.wait()


def slots_kernel(place_ref, own_ref, other_ref, out_ref):
    rows = own_ref.shape[0] - ID_ROWS
    late = place_ref[0] == 1
    index = place_ref[1]
    for slot in range(out_ref.shape[0]):
        wanted = jnp.logical_and(late, index > slot)
        out_ref[slot, :rows] = jnp.where(wanted, other_ref[:rows], own_ref[:rows])
        out_ref[slot, rows:, :HD] = own_ref[rows:, :HD]
        out_ref[slot, rows:, HD:] = other_ref[rows:, HD:]


def vision_kernel(place_ref, keys_ref, values_ref, gain_ref, kept_ref, swapped_ref):
    turns = kept_ref.shape[0]
    core = lax.rem(place_ref[2], 2)
    for turn in range(turns):
        pair = lax.rem(place_ref[2] // 2 + turn, turns)
        for out_ref, side in ((kept_ref, core), (swapped_ref, 1 - core)):
            columns = pl.ds(pl.multiple_of((2 * pair + side) * HD, HD), HD)
            out_ref[turn, :, :HD] = rms_scale(keys_ref[:, columns], gain_ref[...]).astype(jnp.bfloat16)
            out_ref[turn, :, HD:] = values_ref[:, columns]


def select_kernel(place_ref, firsts_ref, slot_ref, *refs):
    *row_refs, out_ref, held = refs
    turns = len(row_refs)
    for turn, row_ref in enumerate(row_refs):
        held[turn] = row_ref[...]
    pair = place_ref[2] // 2
    core = lax.rem(place_ref[2], 2)
    for index in range(out_ref.shape[0]):
        for offset in range(2):
            slot = slot_ref[jnp.minimum(firsts_ref[index] + offset, slot_ref.shape[0] - 1)]
            turn = lax.rem(pair - slot // 2 + turns, turns)
            side = (lax.rem(slot, 2) != core).astype(jnp.int32)
            out_ref[index, offset] = held[turn, side]


def attend_text(q_ref, kv_ref, masked_chunk, other_chunks, allowed_of, queries, peaks, totals, sums):
    rows = q_ref.shape[0]
    heads = q_ref.shape[1] // HD
    width = CHUNK * rows
    for head in range(heads):
        queries[head] = split_scaled(q_ref[:, head_columns(head)])

    def load(chunk):
        blocks = pl.ds(chunk * CHUNK, CHUNK)
        keys = kv_ref[blocks, :rows, :HD].reshape(width, HD)
        values = kv_ref[blocks, :rows, HD:].reshape(width, HD)
        return (
            jnp.concatenate([keys, keys], axis=1),
            jnp.concatenate([values, jnp.ones_like(values)], axis=1),
        )

    masked_keys, masked_values = load(masked_chunk)
    row_index = lax.broadcasted_iota(jnp.int32, (rows, width), 0)
    column = lax.broadcasted_iota(jnp.int32, (rows, width), 1) + masked_chunk * width
    allowed = allowed_of(row_index, column)

    def first_scores(head):
        return jnp.where(allowed, rows_dot(queries[head], masked_keys), MASKED)

    def first_use(head, scores):
        peak = row_peak(scores)
        powers = jnp.exp2(scores - tile_lanes(peak, width)).astype(jnp.bfloat16)
        mixed = dot(powers, masked_values)
        peaks[head] = peak
        sums[head] = mixed[:, :HD]
        totals[head] = mixed[:, HD:]

    pipelined(heads, first_scores, first_use)

    def step(turn, carry):
        keys, values = load(turn + (turn >= masked_chunk).astype(jnp.int32))

        def scores_of(head):
            return rows_dot(queries[head], keys)

        def use(head, scores):
            old_peak = peaks[head]
            peak = jnp.maximum(old_peak, row_peak(scores))
            powers = jnp.exp2(scores - tile_lanes(peak, width)).astype(jnp.bfloat16)
            factor = jnp.exp2(old_peak - peak)
            mixed = dot(powers, values)
            peaks[head] = peak
            sums[head] = sums[head] * factor + mixed[:, :HD]
            totals[head] = totals[head] * factor + mixed[:, HD:]

        pipelined(heads, scores_of, use)
        return carry

    lax.fori_loop(0, other_chunks, step, 0)


def packed_logs(peaks, totals):
    heads, rows, _ = peaks.shape
    owner = lax.rem(lax.broadcasted_iota(jnp.int32, (rows, HD), 1), heads)
    peak, total = peaks[0], totals[0]
    for head in range(1, heads):
        peak = jnp.where(owner == head, peaks[head], peak)
        total = jnp.where(owner == head, totals[head], total)
    return peak + jnp.log2(total)


def first_kernel(place_ref, own_q_ref, sent_q_ref, kv_ref, out_ref, logs_ref, ship_ref, queries, peaks, totals, sums):
    rows = own_q_ref.shape[0]
    heads = own_q_ref.shape[1] // HD
    slots = kv_ref.shape[0]
    index = place_ref[1]
    state = (queries, peaks, totals, sums)

    @pl.when(place_ref[0] == 1)
    def _():
        def allowed(row, column):
            return jnp.logical_or(column <= row + index * rows, column >= (index + 1) * rows)

        attend_text(own_q_ref, kv_ref, index // CHUNK, slots // CHUNK - 1, allowed, *state)
        for head in range(heads):
            out_ref[:, head_columns(head)] = sums[head] / totals[head]
        logs_ref[...] = packed_logs(peaks, totals)

    @pl.when(place_ref[0] == 0)
    def _():
        count = slots - index

        def allowed(row, column):
            return column < count * rows

        attend_text(sent_q_ref, kv_ref, (count - 1) // CHUNK, (count - 1) // CHUNK, allowed, *state)
        for head in range(heads):
            ship_ref[:, head_columns(head)] = (sums[head] / totals[head]).astype(jnp.bfloat16)
        logs = packed_logs(peaks, totals)
        high = logs.astype(jnp.bfloat16).astype(jnp.float32)
        middle = (logs - high).astype(jnp.bfloat16).astype(jnp.float32)
        low = logs - high - middle
        lane = lax.broadcasted_iota(jnp.int32, (rows, HD), 1)
        coded = jnp.where(lane < heads, high, jnp.where(lane < 2 * heads, middle, low))
        ship_ref[:, heads * HD :] = coded.astype(jnp.bfloat16)


def run_start(ids_ref, image):
    count = ids_ref.shape[0]
    start = jnp.int32(0)
    step = count // 2
    while step:
        start = jnp.where(ids_ref[start + step - 1] < image, start + step, start)
        step //= 2
    return start + (ids_ref[start] < image).astype(jnp.int32)


def second_kernel(
    place_ref,
    ids_ref,
    text_q_ref,
    text_kv_ref,
    cross_q_ref,
    gain_ref,
    gate_ref,
    image_kv_ref,
    out_ref,
    queries,
    peaks,
    totals,
    sums,
):
    rows = text_q_ref.shape[0]
    heads = text_q_ref.shape[1] // HD
    index = place_ref[1]

    @pl.when(place_ref[0] == 0)
    def _():
        def allowed(row, column):
            return column <= row + index * rows

        attend_text(text_q_ref, text_kv_ref, index // CHUNK, index // CHUNK, allowed, queries, peaks, totals, sums)
        for head in range(heads):
            out_ref[:, head_columns(head)] = sums[head] / totals[head]

    @pl.when(place_ref[0] == 1)
    def _():
        out_ref[...] = jnp.zeros_like(out_ref)

    sources, _, part, _ = image_kv_ref.shape
    width = sources * part
    first = jnp.maximum(ids_ref[0], 0)
    last = ids_ref[rows - 1]
    gates = jnp.tanh(gate_ref[...])

    @pl.when(last >= first)
    def _():
        for head in range(heads):
            normed = rms_scale(cross_q_ref[:, head_columns(head)], gain_ref[...]).astype(jnp.bfloat16)
            queries[head] = split_scaled(normed)

    def attend(offset):
        keys = image_kv_ref[:, offset, :, :HD].reshape(width, HD)
        values = image_kv_ref[:, offset, :, HD:].reshape(width, HD)
        keys = jnp.concatenate([keys, keys], axis=1)
        values = jnp.concatenate([values, jnp.ones_like(values)], axis=1)
        row = lax.broadcasted_iota(jnp.int32, (rows, HD), 0)
        begin = run_start(ids_ref, first + offset)
        end = run_start(ids_ref, first + offset + 1)
        matches = jnp.logical_and(row >= begin, row < end)

        def scores_of(head):
            return rows_dot(queries[head], keys)

        def use(head, scores):
            powers = jnp.exp2(scores - tile_lanes(row_peak(scores), width)).astype(jnp.bfloat16)
            mixed = dot(powers, values)
            attended = mixed[:, :HD] / mixed[:, HD:]
            gated = jnp.where(matches, gates[head : head + 1] * attended, 0.0)
            out_ref[:, head_columns(head)] = out_ref[:, head_columns(head)] + gated

        pipelined(heads, scores_of, use)

    for offset in range(2):
        pl.when(last >= first + offset)(functools.partial(attend, offset))


def final_kernel(place_ref, base_ref, late_ref, logs_ref, sent_ref, down_ref, out_ref, rank_ref):
    rows, width = base_ref.shape
    heads = width // HD

    @pl.when(place_ref[0] == 0)
    def _():
        out_ref[...] = base_ref[...].astype(jnp.bfloat16)

    @pl.when(place_ref[0] == 1)
    def _():
        coded = sent_ref[:, width:].astype(jnp.float32)
        sent_logs = coded + pltpu.roll(coded, HD - heads, 1) + pltpu.roll(coded, HD - 2 * heads, 1)
        own_logs = logs_ref[...]
        peak = jnp.maximum(own_logs, sent_logs)
        own_part = jnp.exp2(own_logs - peak)
        sent_part = jnp.exp2(sent_logs - peak)
        own_part = own_part / (own_part + sent_part)
        sent_part = 1.0 - own_part
        for head in range(heads):
            columns = head_columns(head)
            mixed = own_part[:, head : head + 1] * late_ref[:, columns]
            mixed = mixed + sent_part[:, head : head + 1] * sent_ref[:, columns].astype(jnp.float32)
            out_ref[:, columns] = (mixed + base_ref[:, columns]).astype(jnp.bfloat16)

    rank = dot(out_ref[...], down_ref[...]).astype(jnp.bfloat16)
    kept = rank_ref.shape[1] // 2
    rank_ref[...] = jnp.concatenate([rank[: rows // 2, :kept], rank[rows // 2 :, :kept]], axis=1)


def swap_cores(values):
    vis = lax.axis_size("vis")
    return lax.ppermute(values, "vis", [(v, v ^ 1) for v in range(vis)])


def turn_pairs(values, turn):
    vis = lax.axis_size("vis")
    return lax.ppermute(values, "vis", [(v, (v + 2 * turn) % vis) for v in range(vis)])


def local(
    text_q,
    text_k,
    text_v,
    cross_q,
    vision_k,
    vision_v,
    q_gain,
    k_gain,
    head_gate,
    adapter_down,
    image_ids,
    image_slot,
):
    rows, q_width = text_q.shape
    heads = q_width // HD
    ctx = lax.axis_size("ctx")
    vis = lax.axis_size("vis")
    half = ctx // 2
    part = vision_k.shape[1]
    small = pltpu.CompilerParams(vmem_limit_bytes=8 * 2**20)
    large = pltpu.CompilerParams(vmem_limit_bytes=24 * 2**20)
    index = lax.axis_index("ctx").astype(jnp.int32)
    place = jnp.stack([index // half, index % half, lax.axis_index("vis").astype(jnp.int32)])
    shape = jax.ShapeDtypeStruct

    payload = pl.pallas_call(
        payload_kernel,
        out_shape=shape((rows + ID_ROWS, 2 * HD), jnp.bfloat16),
        in_specs=[SMEM, HBM, HBM],
        out_specs=VMEM,
        scratch_shapes=[pltpu.SemaphoreType.DMA, pltpu.SemaphoreType.DMA],
        compiler_params=small,
    )(image_ids, text_k, text_v)
    other = lax.ppermute(payload, "ctx", [(c, (c + half) % ctx) for c in range(ctx)])
    outgoing = pl.pallas_call(
        slots_kernel,
        out_shape=shape((half,) + payload.shape, jnp.bfloat16),
        in_specs=[SMEM, VMEM, VMEM],
        out_specs=VMEM,
        compiler_params=small,
    )(place, payload, other)
    planes = [list(range(half)), list(range(half, ctx))]
    text_kv = lax.all_to_all(outgoing, "ctx", 0, 0, axis_index_groups=planes)

    pairs = vis // 2
    kept, swapped = pl.pallas_call(
        vision_kernel,
        out_shape=[shape((pairs, part, 2 * HD), jnp.bfloat16)] * 2,
        in_specs=[SMEM] + [VMEM] * 3,
        out_specs=[VMEM] * 2,
        compiler_params=small,
    )(place, vision_k[0], vision_v[0], k_gain.reshape(1, HD))
    down = jnp.pad(adapter_down, ((0, 0), (0, HD - adapter_down.shape[1])))
    gates = jnp.broadcast_to(head_gate[:, None], (heads, HD))
    kept, swapped, down, gates, text_queries, _ = lax.optimization_barrier(
        (kept, swapped, down, gates, text_q, outgoing)
    )
    sent_q = lax.ppermute(text_queries, "ctx", [(c, ctx - 1 - c) for c in range(half, ctx)])
    both = jnp.stack([kept, swap_cores(swapped)], axis=1)
    slots_kv = [both[0]] + [turn_pairs(both[turn], turn) for turn in range(1, pairs)]

    same = text_kv[:, rows, 0]
    across = text_kv[:, rows, HD]
    late = index >= half
    firsts = jnp.concatenate([jnp.where(late, across, same), jnp.where(late, same, across)]).astype(jnp.int32)
    firsts, sent_q = lax.optimization_barrier((firsts, sent_q))
    picked = pl.pallas_call(
        select_kernel,
        out_shape=shape((ctx, 2, part, 2 * HD), jnp.bfloat16),
        in_specs=[SMEM] * 3 + [VMEM] * pairs,
        out_specs=VMEM,
        scratch_shapes=[pltpu.VMEM((pairs, 2, part, 2 * HD), jnp.bfloat16)],
        compiler_params=small,
    )(place, firsts, image_slot, *slots_kv)
    image_kv = lax.all_to_all(picked, "ctx", 0, 0)

    state = pltpu.VMEM((heads, rows, HD), jnp.float32)
    text_scratch = [pltpu.VMEM((heads, rows, 2 * HD), jnp.bfloat16), state, state, state]
    late_att, late_logs, ship = pl.pallas_call(
        first_kernel,
        out_shape=(
            shape((rows, q_width), jnp.float32),
            shape((rows, HD), jnp.float32),
            shape((rows, q_width + HD), jnp.bfloat16),
        ),
        in_specs=[SMEM] + [VMEM] * 3,
        out_specs=(VMEM, VMEM, VMEM),
        scratch_shapes=text_scratch,
        compiler_params=large,
        cost_estimate=pl.CostEstimate(flops=9 * 10**9, bytes_accessed=6 * 10**6, transcendentals=9 * 10**6),
    )(place, text_q, sent_q, text_kv)
    sent = lax.ppermute(ship, "ctx", [(c, ctx - 1 - c) for c in range(half)])
    base = pl.pallas_call(
        second_kernel,
        out_shape=shape((rows, q_width), jnp.float32),
        in_specs=[SMEM] * 2 + [VMEM] * 6,
        out_specs=VMEM,
        scratch_shapes=text_scratch,
        compiler_params=large,
        cost_estimate=pl.CostEstimate(flops=9 * 10**9, bytes_accessed=6 * 10**6, transcendentals=9 * 10**6),
    )(place, image_ids, text_q, text_kv, cross_q, q_gain.reshape(1, HD), gates, image_kv)
    mixed_out, partial = pl.pallas_call(
        final_kernel,
        out_shape=(shape((rows, q_width), jnp.bfloat16), shape((rows // 2, 2 * adapter_down.shape[1]), jnp.bfloat16)),
        in_specs=[SMEM] + [VMEM] * 5,
        out_specs=(VMEM, VMEM),
        compiler_params=large,
    )(place, base, late_att, late_logs, sent, down)
    chip_sum = (partial.astype(jnp.float32) + swap_cores(partial).astype(jnp.float32)).astype(jnp.bfloat16)
    summed = chip_sum.astype(jnp.float32)
    for turn in range(1, pairs):
        summed = summed + turn_pairs(chip_sum, turn).astype(jnp.float32)
    rank = adapter_down.shape[1]
    lowrank = jnp.concatenate([summed[:, :rank], summed[:, rank:]], axis=0)
    return (mixed_out, lowrank)


def solution(mesh):
    return jax.shard_map(
        local,
        mesh=mesh,
        in_specs=(
            P("ctx", "vis"),
            P("ctx", "vis"),
            P("ctx", "vis"),
            P("ctx", "vis"),
            P("vis", "ctx", None),
            P("vis", "ctx", None),
            P(),
            P(),
            P("vis"),
            P("vis", None),
            P("ctx"),
            P(),
        ),
        out_specs=(P("ctx", "vis"), P("ctx", None)),
        check_vma=False,
    )
```

```python
import functools
import math

import jax
import jax.numpy as jnp
from jax import lax
from jax.experimental import pallas as pl
from jax.experimental.pallas import tpu as pltpu
from jax.sharding import PartitionSpec as P

HD = 128
EPSILON = 1e-05
MASKED = -1e30
SCALE = HD**-0.5 / math.log(2.0)
CHUNK = 4
ID_ROWS = 16

VMEM = pl.BlockSpec(memory_space=pltpu.VMEM)
ANY = pl.BlockSpec(memory_space=pl.ANY)
SMEM = pl.BlockSpec(memory_space=pltpu.SMEM)


def rows_dot(left, right):
    return lax.dot_general(left, right, (((1,), (1,)), ((), ())), preferred_element_type=jnp.float32)


def dot(left, right):
    return jnp.dot(left, right, preferred_element_type=jnp.float32)


def rms_scale(values, weights):
    widened = values.astype(jnp.float32)
    mean_sq = jnp.mean(widened * widened, axis=-1, keepdims=True)
    return widened * lax.rsqrt(mean_sq + EPSILON) * weights


def split_scaled(queries):
    scaled = queries.astype(jnp.float32) * SCALE
    high = scaled.astype(jnp.bfloat16)
    low = (scaled - high.astype(jnp.float32)).astype(jnp.bfloat16)
    return jnp.concatenate([high, low], axis=1)


def tile_lanes(rows, width):
    return jnp.concatenate([rows] * (width // HD), axis=1)


def row_peak(scores):
    peak = scores[:, :HD]
    for start in range(HD, scores.shape[1], HD):
        peak = jnp.maximum(peak, scores[:, start : start + HD])
    return jnp.broadcast_to(jnp.max(peak, axis=1, keepdims=True), peak.shape)


def head_columns(head):
    return slice(head * HD, (head + 1) * HD)


def pipelined(heads, scores_of, use):
    scores = scores_of(0)
    for head in range(heads):
        following = scores_of(head + 1) if head + 1 < heads else None
        use(head, scores)
        scores = following


def payload_kernel(keys_ref, values_ref, out_ref):
    out_ref[:, :HD] = keys_ref[...]
    out_ref[:, HD:] = values_ref[...]


def slots_kernel(place_ref, own_ref, other_ref, ids_ref, out_ref):
    rows = own_ref.shape[0]
    late = place_ref[0] == 1
    index = place_ref[1]
    first = jnp.maximum(ids_ref[:1, :1], 0).astype(jnp.float32)
    first = jnp.broadcast_to(first, (ID_ROWS, 2 * HD)).astype(jnp.bfloat16)
    for slot in range(out_ref.shape[0]):
        wanted = jnp.logical_and(late, index > slot)
        out_ref[slot, :rows] = jnp.where(wanted, other_ref[...], own_ref[...])
        out_ref[slot, rows:] = first


def vision_kernel(place_ref, keys_ref, values_ref, gain_ref, kept_ref, swapped_ref):
    turns = kept_ref.shape[0]
    core = lax.rem(place_ref[2], 2)
    for turn in range(turns):
        pair = lax.rem(place_ref[2] // 2 + turn, turns)
        for out_ref, side in ((kept_ref, core), (swapped_ref, 1 - core)):
            columns = pl.ds(pl.multiple_of((2 * pair + side) * HD, HD), HD)
            out_ref[turn, :, :HD] = rms_scale(keys_ref[:, columns], gain_ref[...]).astype(jnp.bfloat16)
            out_ref[turn, :, HD:] = values_ref[:, columns]


def select_kernel(place_ref, firsts_ref, slot_ref, own_ref, other_ref, out_ref, held):
    turns, _, part, _ = own_ref.shape
    images = held.shape[0]
    pair = place_ref[2] // 2
    core = lax.rem(place_ref[2], 2)
    for image in range(images):
        slot = slot_ref[image]
        turn = lax.rem(pair - slot // 2 + turns, turns)
        side = (lax.rem(slot, 2) != core).astype(jnp.int32)
        held[image, :part] = own_ref[turn, side]
        held[image, part:] = other_ref[turn, side]
    for index in range(out_ref.shape[0]):
        first = firsts_ref[index]
        out_ref[index, 0] = held[first]
        out_ref[index, 1] = held[jnp.minimum(first + 1, images - 1)]


def load_chunk(kv_ref, chunk, rows):
    blocks = pl.ds(chunk * CHUNK, CHUNK)
    keys = kv_ref[blocks, :rows, :HD].reshape(CHUNK * rows, HD)
    values = kv_ref[blocks, :rows, HD:].reshape(CHUNK * rows, HD)
    return (
        jnp.concatenate([keys, keys], axis=1),
        jnp.concatenate([values, jnp.ones_like(values)], axis=1),
    )


def start_text(queries, kv_ref, chunk, slope, limit, beyond, peaks, totals, sums):
    heads, rows, _ = queries.shape
    width = CHUNK * rows
    keys, values = load_chunk(kv_ref, chunk, rows)
    row = lax.broadcasted_iota(jnp.int32, (rows, width), 0)
    column = lax.broadcasted_iota(jnp.int32, (rows, width), 1) + chunk * width
    allowed = jnp.logical_or(column <= row * slope + limit, column >= beyond)

    def scores_of(head):
        return jnp.where(allowed, rows_dot(queries[head], keys), MASKED)

    def use(head, scores):
        peak = row_peak(scores)
        powers = jnp.exp2(scores - tile_lanes(peak, width)).astype(jnp.bfloat16)
        mixed = dot(powers, values)
        peaks[head] = peak
        sums[head] = mixed[:, :HD]
        totals[head] = mixed[:, HD:]

    pipelined(heads, scores_of, use)


def continue_text(queries, kv_ref, arrive, begin, end, peaks, totals, sums):
    heads, rows, _ = queries.shape
    width = CHUNK * rows

    def step(chunk, carry):
        arrive(chunk)
        keys, values = load_chunk(kv_ref, chunk, rows)

        def scores_of(head):
            return rows_dot(queries[head], keys)

        def use(head, scores):
            old_peak = peaks[head]
            peak = jnp.maximum(old_peak, row_peak(scores))
            powers = jnp.exp2(scores - tile_lanes(peak, width)).astype(jnp.bfloat16)
            factor = jnp.exp2(old_peak - peak)
            mixed = dot(powers, values)
            peaks[head] = peak
            sums[head] = sums[head] * factor + mixed[:, :HD]
            totals[head] = totals[head] * factor + mixed[:, HD:]

        pipelined(heads, scores_of, use)
        return carry

    lax.fori_loop(begin, end, step, 0)


def chunk_copy(source, held, sems, chunk):
    blocks = pl.ds(chunk * CHUNK, CHUNK)
    return pltpu.make_async_copy(source.at[blocks], held.at[blocks], sems.at[chunk])


def packed_logs(peaks, totals):
    heads, rows, _ = peaks.shape
    owner = lax.rem(lax.broadcasted_iota(jnp.int32, (rows, HD), 1), heads)
    peak, total = peaks[0], totals[0]
    for head in range(1, heads):
        peak = jnp.where(owner == head, peaks[head], peak)
        total = jnp.where(owner == head, totals[head], total)
    return peak + jnp.log2(total)


def first_kernel(
    place_ref,
    own_q_ref,
    sent_q_ref,
    kv_ref,
    out_ref,
    logs_ref,
    ship_ref,
    q_held,
    kv_held,
    queries,
    peaks,
    totals,
    sums,
    q_sem,
    kv_sems,
):
    heads, rows, _ = queries.shape
    chunks = kv_ref.shape[0] // CHUNK
    late = place_ref[0]
    index = place_ref[1]
    count = kv_ref.shape[0] - index
    masked = jnp.where(late == 1, index, count - 1) // CHUNK

    def chunk_of(chunk):
        return chunk_copy(kv_ref, kv_held, kv_sems, chunk)

    @pl.when(late == 1)
    def _():
        pltpu.make_async_copy(own_q_ref, q_held, q_sem).start()

    @pl.when(late == 0)
    def _():
        pltpu.make_async_copy(sent_q_ref, q_held, q_sem).start()

    chunk_of(masked).start()
    for chunk in range(chunks):
        pl.when(chunk < masked)(chunk_of(chunk).start)

    pltpu.make_async_copy(own_q_ref, q_held, q_sem).wait()
    for head in range(heads):
        queries[head] = split_scaled(q_held[:, head_columns(head)])
    limit = jnp.where(late == 1, index * rows, count * rows - 1)
    beyond = jnp.where(late == 1, (index + 1) * rows, kv_ref.shape[0] * rows)
    chunk_of(masked).wait()
    start_text(queries, kv_held, masked, late, limit, beyond, peaks, totals, sums)
    continue_text(queries, kv_held, lambda chunk: chunk_of(chunk).wait(), 0, masked, peaks, totals, sums)
    logs = packed_logs(peaks, totals)

    @pl.when(late == 1)
    def _():
        for head in range(heads):
            out_ref[:, head_columns(head)] = sums[head] / totals[head]
        logs_ref[...] = logs

    @pl.when(late == 0)
    def _():
        for head in range(heads):
            ship_ref[:, head_columns(head)] = (sums[head] / totals[head]).astype(jnp.bfloat16)
        high = logs.astype(jnp.bfloat16).astype(jnp.float32)
        middle = (logs - high).astype(jnp.bfloat16).astype(jnp.float32)
        low = logs - high - middle
        lane = lax.broadcasted_iota(jnp.int32, (rows, HD), 1)
        coded = jnp.where(lane < heads, high, jnp.where(lane < 2 * heads, middle, low))
        ship_ref[:, heads * HD :] = coded.astype(jnp.bfloat16)


def run_start(ids_ref, image):
    count = ids_ref.shape[0]
    start = jnp.int32(0)
    step = count // 2
    while step:
        start = jnp.where(ids_ref[start + step - 1] < image, start + step, start)
        step //= 2
    return start + (ids_ref[start] < image).astype(jnp.int32)


def second_kernel(
    place_ref,
    q_ref,
    kv_ref,
    early_ref,
    early_logs_ref,
    att_ref,
    logs_ref,
    q_held,
    kv_held,
    early_held,
    early_logs_held,
    queries,
    peaks,
    totals,
    sums,
    sems,
    kv_sems,
):
    heads, rows, _ = queries.shape
    slots = kv_ref.shape[0]
    chunks = slots // CHUNK
    late = place_ref[0]
    index = place_ref[1]
    masked = index // CHUNK
    q_copy = pltpu.make_async_copy(q_ref, q_held, sems.at[0])
    early_copy = pltpu.make_async_copy(early_ref, early_held, sems.at[1])
    logs_copy = pltpu.make_async_copy(early_logs_ref, early_logs_held, sems.at[2])

    def chunk_of(chunk):
        return chunk_copy(kv_ref, kv_held, kv_sems, chunk)

    def arrive(chunk):
        chunk_of(chunk).wait()

    q_copy.start()

    @pl.when(late == 0)
    def _():
        chunk_of(masked).start()
        for chunk in range(chunks):
            pl.when(chunk < masked)(chunk_of(chunk).start)

    @pl.when(late == 1)
    def _():
        logs_copy.start()
        early_copy.start()
        for chunk in range(chunks):
            pl.when(chunk > masked)(chunk_of(chunk).start)

    q_copy.wait()
    for head in range(heads):
        queries[head] = split_scaled(q_held[:, head_columns(head)])

    @pl.when(late == 0)
    def _():
        arrive(masked)
        start_text(queries, kv_held, masked, 1, index * rows, slots * rows, peaks, totals, sums)

    @pl.when(late == 1)
    def _():
        logs_copy.wait()
        early_copy.wait()
        for head in range(heads):
            peaks[head] = jnp.broadcast_to(early_logs_held[:, head : head + 1], (rows, HD))
            totals[head] = jnp.ones_like(totals[head])
            sums[head] = early_held[:, head_columns(head)]

    begin = jnp.where(late == 1, masked + 1, 0)
    end = jnp.where(late == 1, chunks, masked)
    continue_text(queries, kv_held, arrive, begin, end, peaks, totals, sums)
    logs_ref[...] = packed_logs(peaks, totals)
    for head in range(heads):
        att_ref[:, head_columns(head)] = sums[head] / totals[head]


def cross_kernel(ids_ref, q_ref, gain_ref, gate_ref, kv_ref, cross_ref, q_held, kv_held, queries, q_sem, kv_sem):
    heads, rows, _ = queries.shape
    sources, _, part, _ = kv_ref.shape
    width = sources * part
    q_copy = pltpu.make_async_copy(q_ref, q_held, q_sem)
    kv_copy = pltpu.make_async_copy(kv_ref, kv_held, kv_sem)
    q_copy.start()
    kv_copy.start()
    first = jnp.maximum(ids_ref[0], 0)
    last = ids_ref[rows - 1]
    gates = jnp.tanh(gate_ref[...])
    q_copy.wait()

    @pl.when(last >= first)
    def _():
        for head in range(heads):
            normed = rms_scale(q_held[:, head_columns(head)], gain_ref[...]).astype(jnp.bfloat16)
            queries[head] = split_scaled(normed)

    kv_copy.wait()

    def attend(offset):
        keys = kv_held[:, offset, :, :HD].reshape(width, HD)
        values = kv_held[:, offset, :, HD:].reshape(width, HD)
        keys = jnp.concatenate([keys, keys], axis=1)
        values = jnp.concatenate([values, jnp.ones_like(values)], axis=1)
        row = lax.broadcasted_iota(jnp.int32, (rows, HD), 0)
        begin = run_start(ids_ref, first + offset)
        end = run_start(ids_ref, first + offset + 1)
        matches = jnp.logical_and(row >= begin, row < end)

        def scores_of(head):
            return rows_dot(queries[head], keys)

        def use(head, scores):
            powers = jnp.exp2(scores - tile_lanes(row_peak(scores), width)).astype(jnp.bfloat16)
            mixed = dot(powers, values)
            gated = gates[head : head + 1] * (mixed[:, :HD] / mixed[:, HD:])
            columns = head_columns(head)
            cross_ref[:, columns] = jnp.where(matches, gated, 0.0 if offset == 0 else cross_ref[:, columns])

        pipelined(heads, scores_of, use)

    @pl.when(last < first)
    def _():
        cross_ref[...] = jnp.zeros_like(cross_ref)

    for offset in range(2):
        pl.when(last >= first + offset)(functools.partial(attend, offset))


def final_kernel(place_ref, att_ref, logs_ref, cross_ref, sent_ref, down_ref, out_ref, rank_ref):
    rows, width = att_ref.shape
    heads = width // HD

    @pl.when(place_ref[0] == 0)
    def _():
        out_ref[...] = (att_ref[...] + cross_ref[...]).astype(jnp.bfloat16)

    @pl.when(place_ref[0] == 1)
    def _():
        coded = sent_ref[:, width:].astype(jnp.float32)
        sent_logs = coded + pltpu.roll(coded, HD - heads, 1) + pltpu.roll(coded, HD - 2 * heads, 1)
        own_logs = logs_ref[...]
        peak = jnp.maximum(own_logs, sent_logs)
        own_part = jnp.exp2(own_logs - peak)
        sent_part = jnp.exp2(sent_logs - peak)
        whole = own_part + sent_part
        own_part = own_part / whole
        sent_part = sent_part / whole
        for head in range(heads):
            columns = head_columns(head)
            mixed = own_part[:, head : head + 1] * att_ref[:, columns]
            mixed = mixed + sent_part[:, head : head + 1] * sent_ref[:, columns].astype(jnp.float32)
            out_ref[:, columns] = (mixed + cross_ref[:, columns]).astype(jnp.bfloat16)

    rank = dot(out_ref[...], down_ref[...]).astype(jnp.bfloat16)
    kept = rank_ref.shape[1] // 2
    for part in range(2):

        @pl.when(pl.program_id(0) == part)
        def _(part=part):
            rank_ref[:, part * kept : (part + 1) * kept] = rank[:, :kept]


def swap_cores(values):
    vis = lax.axis_size("vis")
    return lax.ppermute(values, "vis", [(v, v ^ 1) for v in range(vis)])


def turn_pairs(values, turn):
    vis = lax.axis_size("vis")
    return lax.ppermute(values, "vis", [(v, (v + 2 * turn) % vis) for v in range(vis)])


def local(
    text_q,
    text_k,
    text_v,
    cross_q,
    vision_k,
    vision_v,
    q_gain,
    k_gain,
    head_gate,
    adapter_down,
    image_ids,
    image_slot,
):
    rows, q_width = text_q.shape
    heads = q_width // HD
    ctx = lax.axis_size("ctx")
    vis = lax.axis_size("vis")
    half = ctx // 2
    part = vision_k.shape[1]
    small = pltpu.CompilerParams(vmem_limit_bytes=8 * 2**20)
    large = pltpu.CompilerParams(vmem_limit_bytes=58 * 2**20)
    index = lax.axis_index("ctx").astype(jnp.int32)
    place = jnp.stack([index // half, index % half, lax.axis_index("vis").astype(jnp.int32)])
    shape = jax.ShapeDtypeStruct

    sent_q = lax.ppermute(text_q, "ctx", [(c, ctx - 1 - c) for c in range(half, ctx)])
    payload = pl.pallas_call(
        payload_kernel,
        out_shape=shape((rows, 2 * HD), jnp.bfloat16),
        in_specs=[VMEM, VMEM],
        out_specs=VMEM,
        compiler_params=small,
    )(text_k, text_v)
    other = lax.ppermute(payload, "ctx", [(c, c + half) for c in range(half)])
    outgoing = pl.pallas_call(
        slots_kernel,
        out_shape=shape((half, rows + ID_ROWS, 2 * HD), jnp.bfloat16),
        in_specs=[SMEM] + [VMEM] * 3,
        out_specs=VMEM,
        compiler_params=small,
    )(place, payload, other, image_ids.reshape(-1, HD))
    outgoing, sent_q = lax.optimization_barrier((outgoing, sent_q))
    planes = [list(range(half)), list(range(half, ctx))]
    text_kv = lax.all_to_all(outgoing, "ctx", 0, 0, axis_index_groups=planes)

    pairs = vis // 2
    kept, swapped = pl.pallas_call(
        vision_kernel,
        out_shape=[shape((pairs, part, 2 * HD), jnp.bfloat16)] * 2,
        in_specs=[SMEM] + [VMEM] * 3,
        out_specs=[VMEM] * 2,
        compiler_params=small,
    )(place, vision_k[0], vision_v[0], k_gain.reshape(1, HD))
    down = jnp.pad(adapter_down, ((0, 0), (0, HD - adapter_down.shape[1])))
    gates = jnp.broadcast_to(head_gate[:, None], (heads, HD))
    kept, swapped, down, gates, _ = lax.optimization_barrier((kept, swapped, down, gates, outgoing))
    both = jnp.stack([kept, swap_cores(swapped)], axis=1)
    slots_kv = jnp.stack([both[0]] + [turn_pairs(both[turn], turn) for turn in range(1, pairs)])
    other_kv = lax.ppermute(slots_kv, "ctx", [(c, (c + half) % ctx) for c in range(ctx)])

    firsts = text_kv[:, rows, 0].astype(jnp.int32)
    picked = pl.pallas_call(
        select_kernel,
        out_shape=shape((half, 2, 2 * part, 2 * HD), jnp.bfloat16),
        in_specs=[SMEM] * 3 + [VMEM] * 2,
        out_specs=VMEM,
        scratch_shapes=[pltpu.VMEM(image_slot.shape + (2 * part, 2 * HD), jnp.bfloat16)],
        compiler_params=small,
    )(place, firsts, image_slot, slots_kv, other_kv)
    image_kv = lax.all_to_all(picked, "ctx", 0, 0, axis_index_groups=planes)

    state = pltpu.VMEM((heads, rows, HD), jnp.float32)
    wide = shape((rows, q_width), jnp.float32)
    logs = shape((rows, HD), jnp.float32)
    cost = pl.CostEstimate(flops=9 * 10**9, bytes_accessed=6 * 10**6, transcendentals=9 * 10**6)
    buffers = [pltpu.VMEM(text_q.shape, text_q.dtype), pltpu.VMEM(text_kv.shape, text_kv.dtype)]
    states = [pltpu.VMEM((heads, rows, 2 * HD), jnp.bfloat16), state, state, state]
    chunk_sems = pltpu.SemaphoreType.DMA((half // CHUNK,))
    early_att, early_logs, ship = pl.pallas_call(
        first_kernel,
        out_shape=(wide, logs, shape((rows, q_width + HD), jnp.bfloat16)),
        in_specs=[SMEM] + [ANY] * 3,
        out_specs=(VMEM, VMEM, VMEM),
        scratch_shapes=buffers + states + [pltpu.SemaphoreType.DMA, chunk_sems],
        compiler_params=large,
        cost_estimate=cost,
    )(place, text_q, sent_q, text_kv)
    sent = lax.ppermute(ship, "ctx", [(c, ctx - 1 - c) for c in range(half)])
    att, att_logs = pl.pallas_call(
        second_kernel,
        out_shape=(wide, logs),
        in_specs=[SMEM] + [ANY] * 4,
        out_specs=(VMEM, VMEM),
        scratch_shapes=buffers
        + [pltpu.VMEM(wide.shape, wide.dtype), pltpu.VMEM(logs.shape, logs.dtype)]
        + states
        + [pltpu.SemaphoreType.DMA((3,)), chunk_sems],
        compiler_params=large,
        cost_estimate=cost,
    )(place, text_q, text_kv, early_att, early_logs)
    crossed = pl.pallas_call(
        cross_kernel,
        out_shape=wide,
        in_specs=[SMEM, ANY, VMEM, VMEM, ANY],
        out_specs=VMEM,
        scratch_shapes=[
            pltpu.VMEM(cross_q.shape, cross_q.dtype),
            pltpu.VMEM(image_kv.shape, image_kv.dtype),
            states[0],
            pltpu.SemaphoreType.DMA,
            pltpu.SemaphoreType.DMA,
        ],
        compiler_params=large,
        cost_estimate=cost,
    )(image_ids, cross_q, q_gain.reshape(1, HD), gates, image_kv)
    rank = adapter_down.shape[1]
    block = rows // 2

    def row_block(columns):
        return pl.BlockSpec((block, columns), lambda turn: (turn, 0))

    def whole(array_shape):
        return pl.BlockSpec(array_shape, lambda turn: (0, 0))

    mixed_out, partial = pl.pallas_call(
        final_kernel,
        grid=(2,),
        out_shape=(shape((rows, q_width), jnp.bfloat16), shape((block, 2 * rank), jnp.bfloat16)),
        in_specs=[SMEM, row_block(q_width), row_block(HD), row_block(q_width), row_block(q_width + HD), whole(down.shape)],
        out_specs=(row_block(q_width), whole((block, 2 * rank))),
        compiler_params=pltpu.CompilerParams(vmem_limit_bytes=12 * 2**20),
    )(place, att, att_logs, crossed, sent, down)
    chip_sum = (partial.astype(jnp.float32) + swap_cores(partial).astype(jnp.float32)).astype(jnp.bfloat16)
    summed = chip_sum.astype(jnp.float32)
    for turn in range(1, pairs):
        summed = summed + turn_pairs(chip_sum, turn).astype(jnp.float32)
    lowrank = jnp.concatenate([summed[:, :rank], summed[:, rank:]], axis=0)
    return (mixed_out, lowrank)


def solution(mesh):
    return jax.shard_map(
        local,
        mesh=mesh,
        in_specs=(
            P("ctx", "vis"),
            P("ctx", "vis"),
            P("ctx", "vis"),
            P("ctx", "vis"),
            P("vis", "ctx", None),
            P("vis", "ctx", None),
            P(),
            P(),
            P("vis"),
            P("vis", None),
            P("ctx"),
            P(),
        ),
        out_specs=(P("ctx", "vis"), P("ctx", None)),
        check_vma=False,
    )
```

```python
import functools
import math

import jax
import jax.numpy as jnp
from jax import lax
from jax.experimental import pallas as pl
from jax.experimental.pallas import tpu as pltpu
from jax.sharding import PartitionSpec as P

HD = 128
EPSILON = 1e-05
MASKED = -1e30
SCALE = HD**-0.5 / math.log(2.0)
CHUNK = 4
PAIR = 2
ID_ROWS = 16

VMEM = pl.BlockSpec(memory_space=pltpu.VMEM)
ANY = pl.BlockSpec(memory_space=pl.ANY)
SMEM = pl.BlockSpec(memory_space=pltpu.SMEM)


def rows_dot(left, right):
    return lax.dot_general(left, right, (((1,), (1,)), ((), ())), preferred_element_type=jnp.float32)


def dot(left, right):
    return jnp.dot(left, right, preferred_element_type=jnp.float32)


def rms_scale(values, weights):
    widened = values.astype(jnp.float32)
    mean_sq = jnp.mean(widened * widened, axis=-1, keepdims=True)
    return widened * lax.rsqrt(mean_sq + EPSILON) * weights


def split_scaled(queries):
    scaled = queries.astype(jnp.float32) * SCALE
    high = scaled.astype(jnp.bfloat16)
    low = (scaled - high.astype(jnp.float32)).astype(jnp.bfloat16)
    return jnp.concatenate([high, low], axis=1)


def tile_lanes(rows, width):
    return jnp.concatenate([rows] * (width // HD), axis=1)


def row_peak(scores):
    peak = scores[:, :HD]
    for start in range(HD, scores.shape[1], HD):
        peak = jnp.maximum(peak, scores[:, start : start + HD])
    return jnp.broadcast_to(jnp.max(peak, axis=1, keepdims=True), peak.shape)


def plane_of(slots):
    ctx = lax.axis_index("ctx")
    return ctx // slots, lax.rem(ctx, slots)


def pair_of():
    vis = lax.axis_index("vis")
    return vis // 2, lax.rem(vis, 2)


def head_columns(head):
    return slice(head * HD, (head + 1) * HD)


def pipelined(heads, scores_of, use):
    groups = [range(start, start + PAIR) for start in range(0, heads, PAIR)]
    scores = [scores_of(head) for head in groups[0]]
    for turn, group in enumerate(groups):
        following = [scores_of(head) for head in groups[turn + 1]] if turn + 1 < len(groups) else None
        use(group, scores)
        scores = following


def weighted(scores, peaks, values):
    powers = [
        jnp.exp2(score - tile_lanes(peak, score.shape[1])).astype(jnp.bfloat16) for score, peak in zip(scores, peaks)
    ]
    mixed = dot(jnp.concatenate(powers, axis=0), values)
    rows = scores[0].shape[0]
    return [mixed[turn * rows : (turn + 1) * rows] for turn in range(len(scores))]


def payload_kernel(keys_ref, values_ref, out_ref):
    out_ref[:, :HD] = keys_ref[...]
    out_ref[:, HD:] = values_ref[...]


def slots_kernel(own_ref, other_ref, ids_ref, out_ref):
    rows = own_ref.shape[0]
    late, index = plane_of(out_ref.shape[0])
    late = late == 1
    first = jnp.maximum(ids_ref[:1, :1], 0).astype(jnp.float32)
    first = jnp.broadcast_to(first, (ID_ROWS, 2 * HD)).astype(jnp.bfloat16)
    for slot in range(out_ref.shape[0]):
        wanted = jnp.logical_and(late, index > slot)
        out_ref[slot, :rows] = jnp.where(wanted, other_ref[...], own_ref[...])
        out_ref[slot, rows:] = first


def vision_kernel(keys_ref, values_ref, gain_ref, kept_ref, swapped_ref):
    turns = kept_ref.shape[0]
    own_pair, core = pair_of()
    for turn in range(turns):
        pair = lax.rem(own_pair + turn, turns)
        for out_ref, side in ((kept_ref, core), (swapped_ref, 1 - core)):
            columns = pl.ds(pl.multiple_of((2 * pair + side) * HD, HD), HD)
            out_ref[turn, :, :HD] = rms_scale(keys_ref[:, columns], gain_ref[...]).astype(jnp.bfloat16)
            out_ref[turn, :, HD:] = values_ref[:, columns]


def select_kernel(firsts_ref, slot_ref, own_ref, other_ref, out_ref, held):
    turns, _, part, _ = own_ref.shape
    images = held.shape[0]
    pair, core = pair_of()
    for image in range(images):
        slot = slot_ref[image]
        turn = lax.rem(pair - slot // 2 + turns, turns)
        side = (lax.rem(slot, 2) != core).astype(jnp.int32)
        held[image, :part] = own_ref[turn, side]
        held[image, part:] = other_ref[turn, side]
    for index in range(out_ref.shape[0]):
        first = firsts_ref[index]
        out_ref[index, 0] = held[first]
        out_ref[index, 1] = held[jnp.minimum(first + 1, images - 1)]


def prepare_kernel(slots, own_ref, sent_ref, cross_ref, gain_ref, first_ref, second_ref, cross_out):
    heads = second_ref.shape[0]
    late, _ = plane_of(slots)
    for head in range(heads):
        columns = head_columns(head)
        second_ref[head] = split_scaled(own_ref[:, columns])
        cross_out[head] = split_scaled(rms_scale(cross_ref[:, columns], gain_ref[...]).astype(jnp.bfloat16))

    @pl.when(late == 1)
    def _():
        first_ref[...] = second_ref[...]

    @pl.when(late == 0)
    def _():
        for head in range(heads):
            first_ref[head] = split_scaled(sent_ref[:, head_columns(head)])


def load_blocks(kv_ref, begin, count, rows):
    blocks = pl.ds(begin, count)
    keys = kv_ref[blocks, :rows, :HD].reshape(count * rows, HD)
    values = kv_ref[blocks, :rows, HD:].reshape(count * rows, HD)
    return (
        jnp.concatenate([keys, keys], axis=1),
        jnp.concatenate([values, jnp.ones_like(values)], axis=1),
    )


def start_text(queries, q_copies, kv_ref, chunk, count, sizes, slope, limit, beyond, peaks, totals, sums):
    heads, rows, _ = queries.shape

    def run(blocks):
        width = blocks * rows
        keys, values = load_blocks(kv_ref, chunk * CHUNK, blocks, rows)
        row = lax.broadcasted_iota(jnp.int32, (rows, width), 0)
        column = lax.broadcasted_iota(jnp.int32, (rows, width), 1) + chunk * (CHUNK * rows)
        allowed = jnp.logical_or(column <= row * slope + limit, column >= beyond)

        def scores_of(head):
            if head % PAIR == 0:
                q_copies[head // PAIR].wait()
            return jnp.where(allowed, rows_dot(queries[head], keys), MASKED)

        def use(group, scores):
            tops = [row_peak(score) for score in scores]
            for head, peak, mixed in zip(group, tops, weighted(scores, tops, values)):
                peaks[head] = peak
                sums[head] = mixed[:, :HD]
                totals[head] = mixed[:, HD:]

        pipelined(heads, scores_of, use)

    for blocks in sizes:
        pl.when(jnp.int32(count) == blocks)(functools.partial(run, blocks))


def continue_text(queries, kv_ref, arrive, begin, end, peaks, totals, sums):
    heads, rows, _ = queries.shape

    def step(chunk, carry):
        arrive(chunk)
        keys, values = load_blocks(kv_ref, chunk * CHUNK, CHUNK, rows)

        def scores_of(head):
            return rows_dot(queries[head], keys)

        def use(group, scores):
            old = [peaks[head] for head in group]
            tops = [jnp.maximum(peak, row_peak(score)) for peak, score in zip(old, scores)]
            for head, before, peak, mixed in zip(group, old, tops, weighted(scores, tops, values)):
                factor = jnp.exp2(before - peak)
                peaks[head] = peak
                sums[head] = sums[head] * factor + mixed[:, :HD]
                totals[head] = totals[head] * factor + mixed[:, HD:]

        pipelined(heads, scores_of, use)
        return carry

    lax.fori_loop(begin, end, step, 0)


def pair_copies(source, held, sems):
    blocks = [pl.ds(start, PAIR) for start in range(0, source.shape[0], PAIR)]
    return [
        pltpu.make_async_copy(source.at[block], held.at[block], sems.at[turn]) for turn, block in enumerate(blocks)
    ]


def chunk_copy(source, held, sems, chunk):
    blocks = pl.ds(chunk * CHUNK, CHUNK)
    return pltpu.make_async_copy(source.at[blocks], held.at[blocks], sems.at[chunk])


def packed_logs(peaks, totals):
    heads, rows, _ = peaks.shape
    owner = lax.rem(lax.broadcasted_iota(jnp.int32, (rows, HD), 1), heads)
    peak, total = peaks[0], totals[0]
    for head in range(1, heads):
        peak = jnp.where(owner == head, peaks[head], peak)
        total = jnp.where(owner == head, totals[head], total)
    return peak + jnp.log2(total)


def first_kernel(
    q_ref,
    kv_ref,
    out_ref,
    logs_ref,
    ship_ref,
    kv_held,
    out_held,
    logs_held,
    ship_held,
    queries,
    peaks,
    totals,
    sums,
    q_sems,
    kv_sems,
    out_sems,
):
    heads, rows, _ = queries.shape
    slots = kv_ref.shape[0]
    late, index = plane_of(slots)
    count = slots - index
    masked = jnp.where(late == 1, index, count - 1) // CHUNK
    q_copies = pair_copies(q_ref, queries, q_sems)

    def chunk_of(chunk):
        return chunk_copy(kv_ref, kv_held, kv_sems, chunk)

    q_copies[0].start()
    chunk_of(masked).start()
    for q_copy in q_copies[1:]:
        q_copy.start()
    for chunk in range(slots // CHUNK):
        pl.when(chunk < masked)(chunk_of(chunk).start)

    sizes = range(1, CHUNK + 1)
    blocks = jnp.where(late == 1, CHUNK, count - masked * CHUNK)
    limit = jnp.where(late == 1, index * rows, count * rows - 1)
    beyond = jnp.where(late == 1, (index + 1) * rows, slots * rows)
    chunk_of(masked).wait()
    start_text(queries, q_copies, kv_held, masked, blocks, sizes, late, limit, beyond, peaks, totals, sums)
    continue_text(queries, kv_held, lambda chunk: chunk_of(chunk).wait(), 0, masked, peaks, totals, sums)
    logs = packed_logs(peaks, totals)

    @pl.when(late == 1)
    def _():
        logs_held[...] = logs
        logs_copy = pltpu.make_async_copy(logs_held, logs_ref, out_sems.at[0])
        logs_copy.start()
        for head in range(heads):
            out_held[:, head_columns(head)] = sums[head] / totals[head]
        out_copy = pltpu.make_async_copy(out_held, out_ref, out_sems.at[1])
        out_copy.start()
        logs_copy.wait()
        out_copy.wait()

    @pl.when(late == 0)
    def _():
        for head in range(heads):
            ship_held[:, head_columns(head)] = (sums[head] / totals[head]).astype(jnp.bfloat16)
        high = logs.astype(jnp.bfloat16).astype(jnp.float32)
        middle = (logs - high).astype(jnp.bfloat16).astype(jnp.float32)
        low = logs - high - middle
        lane = lax.broadcasted_iota(jnp.int32, (rows, HD), 1)
        coded = jnp.where(lane < heads, high, jnp.where(lane < 2 * heads, middle, low))
        ship_held[:, heads * HD :] = coded.astype(jnp.bfloat16)
        ship_copy = pltpu.make_async_copy(ship_held, ship_ref, out_sems.at[2])
        ship_copy.start()
        ship_copy.wait()


def run_start(ids_ref, image):
    count = ids_ref.shape[0]
    start = jnp.int32(0)
    step = count // 2
    while step:
        start = jnp.where(ids_ref[start + step - 1] < image, start + step, start)
        step //= 2
    return start + (ids_ref[start] < image).astype(jnp.int32)


def second_kernel(
    q_ref,
    kv_ref,
    early_ref,
    early_logs_ref,
    att_ref,
    logs_ref,
    kv_held,
    early_held,
    early_logs_held,
    queries,
    peaks,
    totals,
    sums,
    sems,
    q_sems,
    kv_sems,
):
    heads, rows, _ = queries.shape
    slots = kv_ref.shape[0]
    chunks = slots // CHUNK
    late, index = plane_of(slots)
    masked = index // CHUNK
    q_copies = pair_copies(q_ref, queries, q_sems)
    early_copy = pltpu.make_async_copy(early_ref, early_held, sems.at[0])
    logs_copy = pltpu.make_async_copy(early_logs_ref, early_logs_held, sems.at[1])

    def chunk_of(chunk):
        return chunk_copy(kv_ref, kv_held, kv_sems, chunk)

    def arrive(chunk):
        chunk_of(chunk).wait()

    q_copies[0].start()

    @pl.when(late == 0)
    def _():
        chunk_of(masked).start()
        for q_copy in q_copies[1:]:
            q_copy.start()
        for chunk in range(chunks):
            pl.when(chunk < masked)(chunk_of(chunk).start)

    @pl.when(late == 1)
    def _():
        logs_copy.start()
        early_copy.start()
        for q_copy in q_copies[1:]:
            q_copy.start()
        for chunk in range(chunks):
            pl.when(chunk > masked)(chunk_of(chunk).start)

    @pl.when(late == 0)
    def _():
        arrive(masked)
        start_text(queries, q_copies, kv_held, masked, CHUNK, (CHUNK,), 1, index * rows, slots * rows, peaks, totals, sums)

    @pl.when(late == 1)
    def _():
        logs_copy.wait()
        early_copy.wait()
        for head in range(heads):
            peaks[head] = jnp.broadcast_to(early_logs_held[:, head : head + 1], (rows, HD))
            totals[head] = jnp.ones_like(totals[head])
            sums[head] = early_held[:, head_columns(head)]
        for q_copy in q_copies:
            q_copy.wait()

    begin = jnp.where(late == 1, masked + 1, 0)
    end = jnp.where(late == 1, chunks, masked)
    continue_text(queries, kv_held, arrive, begin, end, peaks, totals, sums)
    logs_ref[...] = packed_logs(peaks, totals)
    for head in range(heads):
        att_ref[:, head_columns(head)] = sums[head] / totals[head]


def cross_kernel(ids_ref, q_ref, gate_ref, kv_ref, cross_ref, kv_held, queries, q_sem, kv_sems):
    heads, rows, _ = queries.shape
    sources, images, part, _ = kv_ref.shape
    width = sources * part
    first = jnp.maximum(ids_ref[0], 0)
    last = ids_ref[rows - 1]
    q_copy = pltpu.make_async_copy(q_ref, queries, q_sem)

    def image_copy(offset):
        return pltpu.make_async_copy(kv_ref.at[:, offset], kv_held.at[offset], kv_sems.at[offset])

    q_copy.start()
    for offset in range(images):
        image_copy(offset).start()
    gates = jnp.tanh(gate_ref[...])
    cross_ref[...] = jnp.zeros_like(cross_ref)
    q_copy.wait()

    def attend(offset, carry):
        image_copy(offset).wait()
        keys = kv_held[offset, :, :, :HD].reshape(width, HD)
        values = kv_held[offset, :, :, HD:].reshape(width, HD)
        keys = jnp.concatenate([keys, keys], axis=1)
        values = jnp.concatenate([values, jnp.ones_like(values)], axis=1)
        row = lax.broadcasted_iota(jnp.int32, (rows, HD), 0)
        begin = run_start(ids_ref, first + offset)
        end = run_start(ids_ref, first + offset + 1)
        matches = jnp.logical_and(row >= begin, row < end)

        def scores_of(head):
            return rows_dot(queries[head], keys)

        def use(group, scores):
            tops = [row_peak(score) for score in scores]
            for head, mixed in zip(group, weighted(scores, tops, values)):
                gated = gates[head : head + 1] * (mixed[:, :HD] / mixed[:, HD:])
                columns = head_columns(head)
                cross_ref[:, columns] = jnp.where(matches, gated, cross_ref[:, columns])

        pipelined(heads, scores_of, use)
        return carry

    count = jnp.clip(last - first + 1, 0, images)
    lax.fori_loop(0, count, attend, 0)
    for offset in range(images):
        pl.when(offset >= count)(image_copy(offset).wait)


def final_kernel(slots, att_ref, logs_ref, cross_ref, sent_ref, down_ref, out_ref, rank_ref):
    rows, width = att_ref.shape
    heads = width // HD
    late, _ = plane_of(slots)

    @pl.when(late == 0)
    def _():
        out_ref[...] = (att_ref[...] + cross_ref[...]).astype(jnp.bfloat16)

    @pl.when(late == 1)
    def _():
        coded = sent_ref[:, width:].astype(jnp.float32)
        sent_logs = coded + pltpu.roll(coded, HD - heads, 1) + pltpu.roll(coded, HD - 2 * heads, 1)
        own_logs = logs_ref[...]
        peak = jnp.maximum(own_logs, sent_logs)
        own_part = jnp.exp2(own_logs - peak)
        sent_part = jnp.exp2(sent_logs - peak)
        whole = own_part + sent_part
        own_part = own_part / whole
        sent_part = sent_part / whole
        for head in range(heads):
            columns = head_columns(head)
            mixed = own_part[:, head : head + 1] * att_ref[:, columns]
            mixed = mixed + sent_part[:, head : head + 1] * sent_ref[:, columns].astype(jnp.float32)
            out_ref[:, columns] = (mixed + cross_ref[:, columns]).astype(jnp.bfloat16)

    rank = dot(out_ref[...], down_ref[...]).astype(jnp.bfloat16)
    kept = rank_ref.shape[1] // 2
    for part in range(2):

        @pl.when(pl.program_id(0) == part)
        def _(part=part):
            rank_ref[:, part * kept : (part + 1) * kept] = rank[:, :kept]


def swap_cores(values):
    vis = lax.axis_size("vis")
    return lax.ppermute(values, "vis", [(v, v ^ 1) for v in range(vis)])


def turn_pairs(values, turn):
    vis = lax.axis_size("vis")
    return lax.ppermute(values, "vis", [(v, (v + 2 * turn) % vis) for v in range(vis)])


def local(
    text_q,
    text_k,
    text_v,
    cross_q,
    vision_k,
    vision_v,
    q_gain,
    k_gain,
    head_gate,
    adapter_down,
    image_ids,
    image_slot,
):
    rows, q_width = text_q.shape
    heads = q_width // HD
    ctx = lax.axis_size("ctx")
    vis = lax.axis_size("vis")
    half = ctx // 2
    part = vision_k.shape[1]
    small = pltpu.CompilerParams(vmem_limit_bytes=8 * 2**20)
    large = pltpu.CompilerParams(vmem_limit_bytes=58 * 2**20)
    shape = jax.ShapeDtypeStruct

    sent_q = lax.ppermute(text_q, "ctx", [(c, ctx - 1 - c) for c in range(half, ctx)])
    payload = pl.pallas_call(
        payload_kernel,
        out_shape=shape((rows, 2 * HD), jnp.bfloat16),
        in_specs=[VMEM, VMEM],
        out_specs=VMEM,
        compiler_params=small,
    )(text_k, text_v)
    other = lax.ppermute(payload, "ctx", [(c, c + half) for c in range(half)])
    outgoing = pl.pallas_call(
        slots_kernel,
        out_shape=shape((half, rows + ID_ROWS, 2 * HD), jnp.bfloat16),
        in_specs=[VMEM] * 3,
        out_specs=VMEM,
        compiler_params=small,
    )(payload, other, image_ids.reshape(-1, HD))
    outgoing, sent_q = lax.optimization_barrier((outgoing, sent_q))
    planes = [list(range(half)), list(range(half, ctx))]
    text_kv = lax.all_to_all(outgoing, "ctx", 0, 0, axis_index_groups=planes)

    split = shape((heads, rows, 2 * HD), jnp.bfloat16)
    gates = jnp.broadcast_to(head_gate[:, None], (heads, HD))
    first_split, second_split, cross_split = pl.pallas_call(
        functools.partial(prepare_kernel, half),
        out_shape=(split, split, split),
        in_specs=[VMEM] * 4,
        out_specs=(VMEM, VMEM, VMEM),
        compiler_params=pltpu.CompilerParams(vmem_limit_bytes=16 * 2**20),
    )(text_q, sent_q, cross_q, q_gain.reshape(1, HD))
    pairs = vis // 2
    kept, swapped = pl.pallas_call(
        vision_kernel,
        out_shape=[shape((pairs, part, 2 * HD), jnp.bfloat16)] * 2,
        in_specs=[VMEM] * 3,
        out_specs=[VMEM] * 2,
        compiler_params=small,
    )(vision_k[0], vision_v[0], k_gain.reshape(1, HD))
    down = jnp.pad(adapter_down, ((0, 0), (0, HD - adapter_down.shape[1])))
    kept, swapped, down, gates, _ = lax.optimization_barrier((kept, swapped, down, gates, outgoing))
    both = jnp.stack([kept, swap_cores(swapped)], axis=1)
    slots_kv = jnp.stack([both[0]] + [turn_pairs(both[turn], turn) for turn in range(1, pairs)])
    other_kv = lax.ppermute(slots_kv, "ctx", [(c, (c + half) % ctx) for c in range(ctx)])

    firsts = text_kv[:, rows, 0].astype(jnp.int32)
    picked = pl.pallas_call(
        select_kernel,
        out_shape=shape((half, 2, 2 * part, 2 * HD), jnp.bfloat16),
        in_specs=[SMEM] * 2 + [VMEM] * 2,
        out_specs=VMEM,
        scratch_shapes=[pltpu.VMEM(image_slot.shape + (2 * part, 2 * HD), jnp.bfloat16)],
        compiler_params=small,
    )(firsts, image_slot, slots_kv, other_kv)
    image_kv = lax.all_to_all(picked, "ctx", 0, 0, axis_index_groups=planes)

    state = pltpu.VMEM((heads, rows, HD), jnp.float32)
    wide = shape((rows, q_width), jnp.float32)
    logs = shape((rows, HD), jnp.float32)
    cost = pl.CostEstimate(flops=9 * 10**9, bytes_accessed=6 * 10**6, transcendentals=9 * 10**6)
    buffers = [pltpu.VMEM(text_kv.shape, text_kv.dtype)]
    states = [pltpu.VMEM(split.shape, split.dtype), state, state, state]
    chunk_sems = pltpu.SemaphoreType.DMA((half // CHUNK,))
    pair_sems = pltpu.SemaphoreType.DMA((heads // PAIR,))
    early_att, early_logs, ship = pl.pallas_call(
        first_kernel,
        out_shape=(wide, logs, shape((rows, q_width + HD), jnp.bfloat16)),
        in_specs=[ANY] * 2,
        out_specs=(ANY, ANY, ANY),
        scratch_shapes=buffers
        + [
            pltpu.VMEM(wide.shape, wide.dtype),
            pltpu.VMEM(logs.shape, logs.dtype),
            pltpu.VMEM((rows, q_width + HD), jnp.bfloat16),
        ]
        + states
        + [pair_sems, chunk_sems, pltpu.SemaphoreType.DMA((3,))],
        compiler_params=large,
        cost_estimate=cost,
    )(first_split, text_kv)
    sent = lax.ppermute(ship, "ctx", [(c, ctx - 1 - c) for c in range(half)])
    att, att_logs = pl.pallas_call(
        second_kernel,
        out_shape=(wide, logs),
        in_specs=[ANY] * 4,
        out_specs=(VMEM, VMEM),
        scratch_shapes=buffers
        + [pltpu.VMEM(wide.shape, wide.dtype), pltpu.VMEM(logs.shape, logs.dtype)]
        + states
        + [pltpu.SemaphoreType.DMA((2,)), pair_sems, chunk_sems],
        compiler_params=large,
        cost_estimate=cost,
    )(second_split, text_kv, early_att, early_logs)
    crossed = pl.pallas_call(
        cross_kernel,
        out_shape=wide,
        in_specs=[SMEM, ANY, VMEM, ANY],
        out_specs=VMEM,
        scratch_shapes=[
            pltpu.VMEM((2, half, 2 * part, 2 * HD), image_kv.dtype),
            states[0],
            pltpu.SemaphoreType.DMA,
            pltpu.SemaphoreType.DMA((2,)),
        ],
        compiler_params=pltpu.CompilerParams(vmem_limit_bytes=20 * 2**20),
        cost_estimate=cost,
    )(image_ids, cross_split, gates, image_kv)
    rank = adapter_down.shape[1]
    block = rows // 2

    def row_block(columns):
        return pl.BlockSpec((block, columns), lambda turn: (turn, 0))

    def whole(array_shape):
        return pl.BlockSpec(array_shape, lambda turn: (0, 0))

    mixed_out, partial = pl.pallas_call(
        functools.partial(final_kernel, half),
        grid=(2,),
        out_shape=(shape((rows, q_width), jnp.bfloat16), shape((block, 2 * rank), jnp.bfloat16)),
        in_specs=[row_block(q_width), row_block(HD), row_block(q_width), row_block(q_width + HD), whole(down.shape)],
        out_specs=(row_block(q_width), whole((block, 2 * rank))),
        compiler_params=pltpu.CompilerParams(vmem_limit_bytes=12 * 2**20),
    )(att, att_logs, crossed, sent, down)
    chip_sum = (partial.astype(jnp.float32) + swap_cores(partial).astype(jnp.float32)).astype(jnp.bfloat16)
    summed = chip_sum.astype(jnp.float32)
    for turn in range(1, pairs):
        summed = summed + turn_pairs(chip_sum, turn).astype(jnp.float32)
    lowrank = jnp.concatenate([summed[:, :rank], summed[:, rank:]], axis=0)
    return (mixed_out, lowrank)


def solution(mesh):
    return jax.shard_map(
        local,
        mesh=mesh,
        in_specs=(
            P("ctx", "vis"),
            P("ctx", "vis"),
            P("ctx", "vis"),
            P("ctx", "vis"),
            P("vis", "ctx", None),
            P("vis", "ctx", None),
            P(),
            P(),
            P("vis"),
            P("vis", None),
            P("ctx"),
            P(),
        ),
        out_specs=(P("ctx", "vis"), P("ctx", None)),
        check_vma=False,
    )
```

```python
import functools
import math

import jax
import jax.numpy as jnp
from jax import lax
from jax.experimental import pallas as pl
from jax.experimental.pallas import tpu as pltpu
from jax.sharding import PartitionSpec as P

HD = 128
EPSILON = 1e-05
MASKED = -1e30
SCALE = HD**-0.5 / math.log(2.0)
CHUNK = 4
PAIR = 2
ID_ROWS = 16

VMEM = pl.BlockSpec(memory_space=pltpu.VMEM)
ANY = pl.BlockSpec(memory_space=pl.ANY)
SMEM = pl.BlockSpec(memory_space=pltpu.SMEM)


def rows_dot(left, right):
    return lax.dot_general(left, right, (((1,), (1,)), ((), ())), preferred_element_type=jnp.float32)


def dot(left, right):
    return jnp.dot(left, right, preferred_element_type=jnp.float32)


def rms_scale(values, weights):
    widened = values.astype(jnp.float32)
    mean_sq = jnp.mean(widened * widened, axis=-1, keepdims=True)
    return widened * lax.rsqrt(mean_sq + EPSILON) * weights


def split_scaled(queries):
    scaled = queries.astype(jnp.float32) * SCALE
    high = scaled.astype(jnp.bfloat16)
    low = (scaled - high.astype(jnp.float32)).astype(jnp.bfloat16)
    return jnp.concatenate([high, low], axis=1)


def tile_lanes(rows, width):
    return jnp.concatenate([rows] * (width // HD), axis=1)


def row_peak(scores):
    peak = scores[:, :HD]
    for start in range(HD, scores.shape[1], HD):
        peak = jnp.maximum(peak, scores[:, start : start + HD])
    return jnp.broadcast_to(jnp.max(peak, axis=1, keepdims=True), peak.shape)


def plane_of(slots):
    ctx = lax.axis_index("ctx")
    return ctx // slots, lax.rem(ctx, slots)


def pair_of():
    vis = lax.axis_index("vis")
    return vis // 2, lax.rem(vis, 2)


def head_columns(head):
    return slice(head * HD, (head + 1) * HD)


def pipelined(heads, scores_of, use):
    groups = [range(start, start + PAIR) for start in range(0, heads, PAIR)]
    scores = [scores_of(head) for head in groups[0]]
    for turn, group in enumerate(groups):
        following = [scores_of(head) for head in groups[turn + 1]] if turn + 1 < len(groups) else None
        use(group, scores)
        scores = following


def weighted(scores, peaks, values):
    powers = [
        jnp.exp2(score - tile_lanes(peak, score.shape[1])).astype(jnp.bfloat16) for score, peak in zip(scores, peaks)
    ]
    mixed = dot(jnp.concatenate(powers, axis=0), values)
    rows = scores[0].shape[0]
    return [mixed[turn * rows : (turn + 1) * rows] for turn in range(len(scores))]


def payload_kernel(keys_ref, values_ref, out_ref):
    out_ref[:, :HD] = keys_ref[...]
    out_ref[:, HD:] = values_ref[...]


def slots_kernel(own_ref, other_ref, ids_ref, out_ref):
    rows = own_ref.shape[0]
    late, index = plane_of(out_ref.shape[0])
    late = late == 1
    first = jnp.maximum(ids_ref[:1, :1], 0).astype(jnp.float32)
    first = jnp.broadcast_to(first, (ID_ROWS, 2 * HD)).astype(jnp.bfloat16)
    for slot in range(out_ref.shape[0]):
        wanted = jnp.logical_and(late, index > slot)
        out_ref[slot, :rows] = jnp.where(wanted, other_ref[...], own_ref[...])
        out_ref[slot, rows:] = first


def vision_kernel(keys_ref, values_ref, gain_ref, kept_ref, swapped_ref):
    turns = kept_ref.shape[0]
    own_pair, core = pair_of()
    for turn in range(turns):
        pair = lax.rem(own_pair + turn, turns)
        for out_ref, side in ((kept_ref, core), (swapped_ref, 1 - core)):
            columns = pl.ds(pl.multiple_of((2 * pair + side) * HD, HD), HD)
            out_ref[turn, :, :HD] = rms_scale(keys_ref[:, columns], gain_ref[...]).astype(jnp.bfloat16)
            out_ref[turn, :, HD:] = values_ref[:, columns]


def select_kernel(firsts_ref, slot_ref, own_ref, other_ref, out_ref, held):
    turns, _, part, _ = own_ref.shape
    images = held.shape[0]
    pair, core = pair_of()
    for image in range(images):
        slot = slot_ref[image]
        turn = lax.rem(pair - slot // 2 + turns, turns)
        side = (lax.rem(slot, 2) != core).astype(jnp.int32)
        held[image, :part] = own_ref[turn, side]
        held[image, part:] = other_ref[turn, side]
    for index in range(out_ref.shape[0]):
        first = firsts_ref[index]
        out_ref[index, 0] = held[first]
        out_ref[index, 1] = held[jnp.minimum(first + 1, images - 1)]


def prepare_kernel(slots, own_ref, sent_ref, cross_ref, gain_ref, first_ref, second_ref, cross_out):
    heads = second_ref.shape[0]
    late, _ = plane_of(slots)
    for head in range(heads):
        columns = head_columns(head)
        second_ref[head] = split_scaled(own_ref[:, columns])
        cross_out[head] = split_scaled(rms_scale(cross_ref[:, columns], gain_ref[...]).astype(jnp.bfloat16))

    @pl.when(late == 1)
    def _():
        first_ref[...] = second_ref[...]

    @pl.when(late == 0)
    def _():
        for head in range(heads):
            first_ref[head] = split_scaled(sent_ref[:, head_columns(head)])


def load_blocks(kv_ref, begin, count, rows):
    blocks = pl.ds(begin, count)
    keys = kv_ref[blocks, :rows, :HD].reshape(count * rows, HD)
    values = kv_ref[blocks, :rows, HD:].reshape(count * rows, HD)
    return (
        jnp.concatenate([keys, keys], axis=1),
        jnp.concatenate([values, jnp.ones_like(values)], axis=1),
    )


def start_text(queries, q_copies, kv_ref, chunk, count, sizes, slope, limit, beyond, peaks, totals, sums):
    heads, rows, _ = queries.shape

    def run(blocks):
        width = blocks * rows
        keys, values = load_blocks(kv_ref, chunk * CHUNK, blocks, rows)
        row = lax.broadcasted_iota(jnp.int32, (rows, width), 0)
        column = lax.broadcasted_iota(jnp.int32, (rows, width), 1) + chunk * (CHUNK * rows)
        allowed = jnp.logical_or(column <= row * slope + limit, column >= beyond)

        def scores_of(head):
            if head % PAIR == 0:
                q_copies[head // PAIR].wait()
            return jnp.where(allowed, rows_dot(queries[head], keys), MASKED)

        def use(group, scores):
            tops = [row_peak(score) for score in scores]
            for head, peak, mixed in zip(group, tops, weighted(scores, tops, values)):
                peaks[head] = peak
                sums[head] = mixed[:, :HD]
                totals[head] = mixed[:, HD:]

        pipelined(heads, scores_of, use)

    for blocks in sizes:
        pl.when(jnp.int32(count) == blocks)(functools.partial(run, blocks))


def add_blocks(queries, keys, values, peaks, totals, sums):
    def scores_of(head):
        return rows_dot(queries[head], keys)

    def use(group, scores):
        old = [peaks[head] for head in group]
        tops = [jnp.maximum(peak, row_peak(score)) for peak, score in zip(old, scores)]
        for head, before, peak, mixed in zip(group, old, tops, weighted(scores, tops, values)):
            factor = jnp.exp2(before - peak)
            peaks[head] = peak
            sums[head] = sums[head] * factor + mixed[:, :HD]
            totals[head] = totals[head] * factor + mixed[:, HD:]

    pipelined(queries.shape[0], scores_of, use)


def continue_text(queries, kv_ref, arrive, begin, end, peaks, totals, sums):
    def step(chunk, carry):
        arrive(chunk)
        keys, values = load_blocks(kv_ref, chunk * CHUNK, CHUNK, queries.shape[1])
        add_blocks(queries, keys, values, peaks, totals, sums)
        return carry

    lax.fori_loop(begin, end, step, 0)


def pair_copies(source, held, sems):
    blocks = [pl.ds(start, PAIR) for start in range(0, source.shape[0], PAIR)]
    return [
        pltpu.make_async_copy(source.at[block], held.at[block], sems.at[turn]) for turn, block in enumerate(blocks)
    ]


def chunk_copy(source, held, sems, chunk):
    blocks = pl.ds(chunk * CHUNK, CHUNK)
    return pltpu.make_async_copy(source.at[blocks], held.at[blocks], sems.at[chunk])


def packed_logs(peaks, totals):
    heads, rows, _ = peaks.shape
    owner = lax.rem(lax.broadcasted_iota(jnp.int32, (rows, HD), 1), heads)
    peak, total = peaks[0], totals[0]
    for head in range(1, heads):
        peak = jnp.where(owner == head, peaks[head], peak)
        total = jnp.where(owner == head, totals[head], total)
    return peak + jnp.log2(total)


def first_kernel(
    q_ref,
    kv_ref,
    out_ref,
    logs_ref,
    ship_ref,
    kv_held,
    out_held,
    logs_held,
    ship_held,
    queries,
    peaks,
    totals,
    sums,
    q_sems,
    kv_sems,
    out_sems,
):
    heads, rows, _ = queries.shape
    slots = kv_ref.shape[0]
    late, index = plane_of(slots)
    count = slots - 1 - index
    masked = jnp.where(late == 1, index, jnp.maximum(count - 1, 0)) // CHUNK
    q_copies = pair_copies(q_ref, queries, q_sems)

    def chunk_of(chunk):
        return chunk_copy(kv_ref, kv_held, kv_sems, chunk)

    q_copies[0].start()
    chunk_of(masked).start()
    for q_copy in q_copies[1:]:
        q_copy.start()
    for chunk in range(slots // CHUNK):
        pl.when(chunk < masked)(chunk_of(chunk).start)

    sizes = range(1, CHUNK + 1)
    blocks = jnp.where(late == 1, CHUNK, jnp.maximum(count, 1) - masked * CHUNK)
    limit = jnp.where(late == 1, index * rows, count * rows - 1)
    beyond = jnp.where(late == 1, (index + 1) * rows, slots * rows)
    chunk_of(masked).wait()
    start_text(queries, q_copies, kv_held, masked, blocks, sizes, late, limit, beyond, peaks, totals, sums)
    continue_text(queries, kv_held, lambda chunk: chunk_of(chunk).wait(), 0, masked, peaks, totals, sums)
    logs = packed_logs(peaks, totals)

    @pl.when(late == 1)
    def _():
        logs_held[...] = logs
        logs_copy = pltpu.make_async_copy(logs_held, logs_ref, out_sems.at[0])
        logs_copy.start()
        for head in range(heads):
            out_held[:, head_columns(head)] = sums[head] / totals[head]
        out_copy = pltpu.make_async_copy(out_held, out_ref, out_sems.at[1])
        out_copy.start()
        logs_copy.wait()
        out_copy.wait()

    @pl.when(late == 0)
    def _():
        for head in range(heads):
            ship_held[:, head_columns(head)] = (sums[head] / totals[head]).astype(jnp.bfloat16)
        high = logs.astype(jnp.bfloat16).astype(jnp.float32)
        middle = (logs - high).astype(jnp.bfloat16).astype(jnp.float32)
        low = logs - high - middle
        lane = lax.broadcasted_iota(jnp.int32, (rows, HD), 1)
        coded = jnp.where(lane < heads, high, jnp.where(lane < 2 * heads, middle, low))
        ship_held[:, heads * HD :] = coded.astype(jnp.bfloat16)
        ship_copy = pltpu.make_async_copy(ship_held, ship_ref, out_sems.at[2])
        ship_copy.start()
        ship_copy.wait()


def run_start(ids_ref, image):
    count = ids_ref.shape[0]
    start = jnp.int32(0)
    step = count // 2
    while step:
        start = jnp.where(ids_ref[start + step - 1] < image, start + step, start)
        step //= 2
    return start + (ids_ref[start] < image).astype(jnp.int32)


def second_kernel(
    q_ref,
    kv_ref,
    early_ref,
    early_logs_ref,
    extra_ref,
    att_ref,
    logs_ref,
    kv_held,
    early_held,
    early_logs_held,
    extra_held,
    queries,
    peaks,
    totals,
    sums,
    sems,
    q_sems,
    kv_sems,
):
    heads, rows, _ = queries.shape
    slots = kv_ref.shape[0]
    chunks = slots // CHUNK
    late, index = plane_of(slots)
    masked = index // CHUNK
    q_copies = pair_copies(q_ref, queries, q_sems)
    early_copy = pltpu.make_async_copy(early_ref, early_held, sems.at[0])
    logs_copy = pltpu.make_async_copy(early_logs_ref, early_logs_held, sems.at[1])
    extra_copy = pltpu.make_async_copy(extra_ref, extra_held.at[0], sems.at[2])

    def chunk_of(chunk):
        return chunk_copy(kv_ref, kv_held, kv_sems, chunk)

    def arrive(chunk):
        chunk_of(chunk).wait()

    q_copies[0].start()

    @pl.when(late == 0)
    def _():
        chunk_of(masked).start()
        for q_copy in q_copies[1:]:
            q_copy.start()
        for chunk in range(chunks):
            pl.when(chunk < masked)(chunk_of(chunk).start)

    @pl.when(late == 1)
    def _():
        logs_copy.start()
        early_copy.start()
        extra_copy.start()
        for q_copy in q_copies[1:]:
            q_copy.start()
        for chunk in range(chunks):
            pl.when(chunk > masked)(chunk_of(chunk).start)

    @pl.when(late == 0)
    def _():
        arrive(masked)
        start_text(queries, q_copies, kv_held, masked, CHUNK, (CHUNK,), 1, index * rows, slots * rows, peaks, totals, sums)

    @pl.when(late == 1)
    def _():
        logs_copy.wait()
        early_copy.wait()
        for head in range(heads):
            peaks[head] = jnp.broadcast_to(early_logs_held[:, head : head + 1], (rows, HD))
            totals[head] = jnp.ones_like(totals[head])
            sums[head] = early_held[:, head_columns(head)]
        for q_copy in q_copies:
            q_copy.wait()
        extra_copy.wait()
        add_blocks(queries, *load_blocks(extra_held, 0, 1, rows), peaks, totals, sums)

    begin = jnp.where(late == 1, masked + 1, 0)
    end = jnp.where(late == 1, chunks, masked)
    continue_text(queries, kv_held, arrive, begin, end, peaks, totals, sums)
    logs_ref[...] = packed_logs(peaks, totals)
    for head in range(heads):
        att_ref[:, head_columns(head)] = sums[head] / totals[head]


def cross_kernel(ids_ref, q_ref, gate_ref, kv_ref, cross_ref, kv_held, queries, q_sem, kv_sems):
    heads, rows, _ = queries.shape
    sources, images, part, _ = kv_ref.shape
    width = sources * part
    first = jnp.maximum(ids_ref[0], 0)
    last = ids_ref[rows - 1]
    q_copy = pltpu.make_async_copy(q_ref, queries, q_sem)

    def image_copy(offset):
        return pltpu.make_async_copy(kv_ref.at[:, offset], kv_held.at[offset], kv_sems.at[offset])

    q_copy.start()
    for offset in range(images):
        image_copy(offset).start()
    gates = jnp.tanh(gate_ref[...])
    cross_ref[...] = jnp.zeros_like(cross_ref)
    q_copy.wait()

    def attend(offset, carry):
        image_copy(offset).wait()
        keys = kv_held[offset, :, :, :HD].reshape(width, HD)
        values = kv_held[offset, :, :, HD:].reshape(width, HD)
        keys = jnp.concatenate([keys, keys], axis=1)
        values = jnp.concatenate([values, jnp.ones_like(values)], axis=1)
        row = lax.broadcasted_iota(jnp.int32, (rows, HD), 0)
        begin = run_start(ids_ref, first + offset)
        end = run_start(ids_ref, first + offset + 1)
        matches = jnp.logical_and(row >= begin, row < end)

        def scores_of(head):
            return rows_dot(queries[head], keys)

        def use(group, scores):
            tops = [row_peak(score) for score in scores]
            for head, mixed in zip(group, weighted(scores, tops, values)):
                gated = gates[head : head + 1] * (mixed[:, :HD] / mixed[:, HD:])
                columns = head_columns(head)
                cross_ref[:, columns] = jnp.where(matches, gated, cross_ref[:, columns])

        pipelined(heads, scores_of, use)
        return carry

    count = jnp.clip(last - first + 1, 0, images)
    lax.fori_loop(0, count, attend, 0)
    for offset in range(images):
        pl.when(offset >= count)(image_copy(offset).wait)


def final_kernel(slots, att_ref, logs_ref, cross_ref, sent_ref, down_ref, out_ref, rank_ref):
    rows, width = att_ref.shape
    heads = width // HD
    late, _ = plane_of(slots)

    @pl.when(late == 0)
    def _():
        out_ref[...] = (att_ref[...] + cross_ref[...]).astype(jnp.bfloat16)

    @pl.when(late == 1)
    def _():
        coded = sent_ref[:, width:].astype(jnp.float32)
        sent_logs = coded + pltpu.roll(coded, HD - heads, 1) + pltpu.roll(coded, HD - 2 * heads, 1)
        own_logs = logs_ref[...]
        peak = jnp.maximum(own_logs, sent_logs)
        own_part = jnp.exp2(own_logs - peak)
        sent_part = jnp.exp2(sent_logs - peak)
        whole = own_part + sent_part
        own_part = own_part / whole
        sent_part = sent_part / whole
        for head in range(heads):
            columns = head_columns(head)
            mixed = own_part[:, head : head + 1] * att_ref[:, columns]
            mixed = mixed + sent_part[:, head : head + 1] * sent_ref[:, columns].astype(jnp.float32)
            out_ref[:, columns] = (mixed + cross_ref[:, columns]).astype(jnp.bfloat16)

    rank_ref[...] = rows_dot(down_ref[...], out_ref[...]).astype(jnp.bfloat16)


def swap_cores(values):
    vis = lax.axis_size("vis")
    return lax.ppermute(values, "vis", [(v, v ^ 1) for v in range(vis)])


def turn_pairs(values, turn):
    vis = lax.axis_size("vis")
    return lax.ppermute(values, "vis", [(v, (v + 2 * turn) % vis) for v in range(vis)])


def local(
    text_q,
    text_k,
    text_v,
    cross_q,
    vision_k,
    vision_v,
    q_gain,
    k_gain,
    head_gate,
    adapter_down,
    image_ids,
    image_slot,
):
    rows, q_width = text_q.shape
    heads = q_width // HD
    ctx = lax.axis_size("ctx")
    vis = lax.axis_size("vis")
    half = ctx // 2
    part = vision_k.shape[1]
    small = pltpu.CompilerParams(vmem_limit_bytes=8 * 2**20)
    large = pltpu.CompilerParams(vmem_limit_bytes=58 * 2**20)
    shape = jax.ShapeDtypeStruct

    sent_q = lax.ppermute(text_q, "ctx", [(c, ctx - 1 - c) for c in range(half, ctx)])
    payload = pl.pallas_call(
        payload_kernel,
        out_shape=shape((rows, 2 * HD), jnp.bfloat16),
        in_specs=[VMEM, VMEM],
        out_specs=VMEM,
        compiler_params=small,
    )(text_k, text_v)
    other = lax.ppermute(payload, "ctx", [(c, c + half) for c in range(half)])
    outgoing = pl.pallas_call(
        slots_kernel,
        out_shape=shape((half, rows + ID_ROWS, 2 * HD), jnp.bfloat16),
        in_specs=[VMEM] * 3,
        out_specs=VMEM,
        compiler_params=small,
    )(payload, other, image_ids.reshape(-1, HD))
    outgoing, sent_q = lax.optimization_barrier((outgoing, sent_q))
    planes = [list(range(half)), list(range(half, ctx))]
    text_kv = lax.all_to_all(outgoing, "ctx", 0, 0, axis_index_groups=planes)

    split = shape((heads, rows, 2 * HD), jnp.bfloat16)
    gates = jnp.broadcast_to(head_gate[:, None], (heads, HD))
    first_split, second_split, cross_split = pl.pallas_call(
        functools.partial(prepare_kernel, half),
        out_shape=(split, split, split),
        in_specs=[VMEM] * 4,
        out_specs=(VMEM, VMEM, VMEM),
        compiler_params=pltpu.CompilerParams(vmem_limit_bytes=16 * 2**20),
    )(text_q, sent_q, cross_q, q_gain.reshape(1, HD))
    pairs = vis // 2
    kept, swapped = pl.pallas_call(
        vision_kernel,
        out_shape=[shape((pairs, part, 2 * HD), jnp.bfloat16)] * 2,
        in_specs=[VMEM] * 3,
        out_specs=[VMEM] * 2,
        compiler_params=small,
    )(vision_k[0], vision_v[0], k_gain.reshape(1, HD))
    down = adapter_down.T
    kept, swapped, down, gates, _ = lax.optimization_barrier((kept, swapped, down, gates, outgoing))
    both = jnp.stack([kept, swap_cores(swapped)], axis=1)
    slots_kv = jnp.stack([both[0]] + [turn_pairs(both[turn], turn) for turn in range(1, pairs)])
    other_kv = lax.ppermute(slots_kv, "ctx", [(c, (c + half) % ctx) for c in range(ctx)])

    firsts = text_kv[:, rows, 0].astype(jnp.int32)
    picked = pl.pallas_call(
        select_kernel,
        out_shape=shape((half, 2, 2 * part, 2 * HD), jnp.bfloat16),
        in_specs=[SMEM] * 2 + [VMEM] * 2,
        out_specs=VMEM,
        scratch_shapes=[pltpu.VMEM(image_slot.shape + (2 * part, 2 * HD), jnp.bfloat16)],
        compiler_params=small,
    )(firsts, image_slot, slots_kv, other_kv)
    image_kv = lax.all_to_all(picked, "ctx", 0, 0, axis_index_groups=planes)

    state = pltpu.VMEM((heads, rows, HD), jnp.float32)
    wide = shape((rows, q_width), jnp.float32)
    logs = shape((rows, HD), jnp.float32)
    cost = pl.CostEstimate(flops=9 * 10**9, bytes_accessed=6 * 10**6, transcendentals=9 * 10**6)
    buffers = [pltpu.VMEM(text_kv.shape, text_kv.dtype)]
    states = [pltpu.VMEM(split.shape, split.dtype), state, state, state]
    chunk_sems = pltpu.SemaphoreType.DMA((half // CHUNK,))
    pair_sems = pltpu.SemaphoreType.DMA((heads // PAIR,))
    early_att, early_logs, ship = pl.pallas_call(
        first_kernel,
        out_shape=(wide, logs, shape((rows, q_width + HD), jnp.bfloat16)),
        in_specs=[ANY] * 2,
        out_specs=(ANY, ANY, ANY),
        scratch_shapes=buffers
        + [
            pltpu.VMEM(wide.shape, wide.dtype),
            pltpu.VMEM(logs.shape, logs.dtype),
            pltpu.VMEM((rows, q_width + HD), jnp.bfloat16),
        ]
        + states
        + [pair_sems, chunk_sems, pltpu.SemaphoreType.DMA((3,))],
        compiler_params=large,
        cost_estimate=cost,
    )(first_split, text_kv)
    sent = lax.ppermute(ship, "ctx", [(c, ctx - 1 - c) for c in range(half)])
    att, att_logs = pl.pallas_call(
        second_kernel,
        out_shape=(wide, logs),
        in_specs=[ANY] * 5,
        out_specs=(VMEM, VMEM),
        scratch_shapes=buffers
        + [pltpu.VMEM(wide.shape, wide.dtype), pltpu.VMEM(logs.shape, logs.dtype), pltpu.VMEM((1,) + other.shape, other.dtype)]
        + states
        + [pltpu.SemaphoreType.DMA((3,)), pair_sems, chunk_sems],
        compiler_params=large,
        cost_estimate=cost,
    )(second_split, text_kv, early_att, early_logs, other)
    crossed = pl.pallas_call(
        cross_kernel,
        out_shape=wide,
        in_specs=[SMEM, ANY, VMEM, ANY],
        out_specs=VMEM,
        scratch_shapes=[
            pltpu.VMEM((2, half, 2 * part, 2 * HD), image_kv.dtype),
            states[0],
            pltpu.SemaphoreType.DMA,
            pltpu.SemaphoreType.DMA((2,)),
        ],
        compiler_params=pltpu.CompilerParams(vmem_limit_bytes=20 * 2**20),
        cost_estimate=cost,
    )(image_ids, cross_split, gates, image_kv)
    rank = adapter_down.shape[1]
    block = rows // 2

    def row_block(columns):
        return pl.BlockSpec((block, columns), lambda turn: (turn, 0))

    def whole(array_shape):
        return pl.BlockSpec(array_shape, lambda turn: (0, 0))

    mixed_out, partial = pl.pallas_call(
        functools.partial(final_kernel, half),
        grid=(2,),
        out_shape=(shape((rows, q_width), jnp.bfloat16), shape((rank, rows), jnp.bfloat16)),
        in_specs=[row_block(q_width), row_block(HD), row_block(q_width), row_block(q_width + HD), whole(down.shape)],
        out_specs=(row_block(q_width), pl.BlockSpec((rank, block), lambda turn: (0, turn))),
        compiler_params=pltpu.CompilerParams(vmem_limit_bytes=12 * 2**20),
    )(att, att_logs, crossed, sent, down)
    chip_sum = (partial.astype(jnp.float32) + swap_cores(partial).astype(jnp.float32)).astype(jnp.bfloat16)
    summed = chip_sum.astype(jnp.float32)
    for turn in range(1, pairs):
        summed = summed + turn_pairs(chip_sum, turn).astype(jnp.float32)
    lowrank = summed.T
    return (mixed_out, lowrank)


def solution(mesh):
    return jax.shard_map(
        local,
        mesh=mesh,
        in_specs=(
            P("ctx", "vis"),
            P("ctx", "vis"),
            P("ctx", "vis"),
            P("ctx", "vis"),
            P("vis", "ctx", None),
            P("vis", "ctx", None),
            P(),
            P(),
            P("vis"),
            P("vis", None),
            P("ctx"),
            P(),
        ),
        out_specs=(P("ctx", "vis"), P("ctx", None)),
        check_vma=False,
    )
```

```python
import functools
import math

import jax
import jax.numpy as jnp
from jax import lax
from jax.experimental import pallas as pl
from jax.experimental.pallas import tpu as pltpu
from jax.sharding import PartitionSpec as P

HD = 128
EPSILON = 1e-05
MASKED = -1e30
SCALE = HD**-0.5 / math.log(2.0)
CHUNK = 4
PAIR = 2
ID_ROWS = 16

VMEM = pl.BlockSpec(memory_space=pltpu.VMEM)
ANY = pl.BlockSpec(memory_space=pl.ANY)
SMEM = pl.BlockSpec(memory_space=pltpu.SMEM)


def rows_dot(left, right):
    return lax.dot_general(left, right, (((1,), (1,)), ((), ())), preferred_element_type=jnp.float32)


def dot(left, right):
    return jnp.dot(left, right, preferred_element_type=jnp.float32)


def rms_scale(values, weights):
    widened = values.astype(jnp.float32)
    mean_sq = jnp.mean(widened * widened, axis=-1, keepdims=True)
    return widened * lax.rsqrt(mean_sq + EPSILON) * weights


def split_scaled(queries):
    scaled = queries.astype(jnp.float32) * SCALE
    high = scaled.astype(jnp.bfloat16)
    low = (scaled - high.astype(jnp.float32)).astype(jnp.bfloat16)
    return jnp.concatenate([high, low], axis=1)


def tile_lanes(rows, width):
    return jnp.concatenate([rows] * (width // HD), axis=1)


def row_peak(scores):
    peak = scores[:, :HD]
    for start in range(HD, scores.shape[1], HD):
        peak = jnp.maximum(peak, scores[:, start : start + HD])
    return jnp.broadcast_to(jnp.max(peak, axis=1, keepdims=True), peak.shape)


def plane_of(slots):
    ctx = lax.axis_index("ctx")
    return ctx // slots, lax.rem(ctx, slots)


def pair_of():
    vis = lax.axis_index("vis")
    return vis // 2, lax.rem(vis, 2)


def head_columns(head):
    return slice(head * HD, (head + 1) * HD)


def pipelined(heads, scores_of, use):
    groups = [range(start, start + PAIR) for start in range(0, heads, PAIR)]
    scores = [scores_of(head) for head in groups[0]]
    for turn, group in enumerate(groups):
        following = [scores_of(head) for head in groups[turn + 1]] if turn + 1 < len(groups) else None
        use(group, scores)
        scores = following


def weighted(scores, peaks, values):
    powers = [
        jnp.exp2(score - tile_lanes(peak, score.shape[1])).astype(jnp.bfloat16) for score, peak in zip(scores, peaks)
    ]
    mixed = dot(jnp.concatenate(powers, axis=0), values)
    rows = scores[0].shape[0]
    return [mixed[turn * rows : (turn + 1) * rows] for turn in range(len(scores))]


def payload_kernel(keys_ref, values_ref, out_ref):
    out_ref[:, :HD] = keys_ref[...]
    out_ref[:, HD:] = values_ref[...]


def slots_kernel(own_ref, other_ref, ids_ref, out_ref):
    rows = own_ref.shape[0]
    late, index = plane_of(out_ref.shape[0])
    late = late == 1
    first = jnp.maximum(ids_ref[:1, :1], 0).astype(jnp.float32)
    first = jnp.broadcast_to(first, (ID_ROWS, 2 * HD)).astype(jnp.bfloat16)
    for slot in range(out_ref.shape[0]):
        wanted = jnp.logical_and(late, index > slot)
        out_ref[slot, :rows] = jnp.where(wanted, other_ref[...], own_ref[...])
        out_ref[slot, rows:] = first


def vision_kernel(keys_ref, values_ref, gain_ref, kept_ref, swapped_ref):
    turns = kept_ref.shape[0]
    own_pair, core = pair_of()
    for turn in range(turns):
        pair = lax.rem(own_pair + turn, turns)
        for out_ref, side in ((kept_ref, core), (swapped_ref, 1 - core)):
            columns = pl.ds(pl.multiple_of((2 * pair + side) * HD, HD), HD)
            out_ref[turn, :, :HD] = rms_scale(keys_ref[:, columns], gain_ref[...]).astype(jnp.bfloat16)
            out_ref[turn, :, HD:] = values_ref[:, columns]


def select_kernel(firsts_ref, slot_ref, own_ref, other_ref, out_ref, held):
    turns, _, part, _ = own_ref.shape
    images = held.shape[0]
    pair, core = pair_of()
    for image in range(images):
        slot = slot_ref[image]
        turn = lax.rem(pair - slot // 2 + turns, turns)
        side = (lax.rem(slot, 2) != core).astype(jnp.int32)
        held[image, :part] = own_ref[turn, side]
        held[image, part:] = other_ref[turn, side]
    for index in range(out_ref.shape[0]):
        first = firsts_ref[index]
        out_ref[index, 0] = held[first]
        out_ref[index, 1] = held[jnp.minimum(first + 1, images - 1)]


def prepare_kernel(slots, own_ref, sent_ref, cross_ref, gain_ref, first_ref, second_ref, cross_out):
    heads = second_ref.shape[0]
    late, _ = plane_of(slots)
    for head in range(heads):
        columns = head_columns(head)
        second_ref[head] = split_scaled(own_ref[:, columns])
        cross_out[head] = split_scaled(rms_scale(cross_ref[:, columns], gain_ref[...]).astype(jnp.bfloat16))

    @pl.when(late == 1)
    def _():
        first_ref[...] = second_ref[...]

    @pl.when(late == 0)
    def _():
        for head in range(heads):
            first_ref[head] = split_scaled(sent_ref[:, head_columns(head)])


def load_blocks(kv_ref, begin, count, rows):
    blocks = pl.ds(begin, count)
    keys = kv_ref[blocks, :rows, :HD].reshape(count * rows, HD)
    values = kv_ref[blocks, :rows, HD:].reshape(count * rows, HD)
    return (
        jnp.concatenate([keys, keys], axis=1),
        jnp.concatenate([values, jnp.ones_like(values)], axis=1),
    )


def start_text(queries, q_copies, kv_ref, chunk, count, sizes, slope, limit, beyond, peaks, totals, sums):
    heads, rows, _ = queries.shape

    def run(blocks):
        width = blocks * rows
        keys, values = load_blocks(kv_ref, chunk * CHUNK, blocks, rows)
        row = lax.broadcasted_iota(jnp.int32, (rows, width), 0)
        column = lax.broadcasted_iota(jnp.int32, (rows, width), 1) + chunk * (CHUNK * rows)
        allowed = jnp.logical_or(column <= row * slope + limit, column >= beyond)

        def scores_of(head):
            if head % PAIR == 0:
                q_copies[head // PAIR].wait()
            return jnp.where(allowed, rows_dot(queries[head], keys), MASKED)

        def use(group, scores):
            tops = [row_peak(score) for score in scores]
            for head, peak, mixed in zip(group, tops, weighted(scores, tops, values)):
                peaks[head] = peak
                sums[head] = mixed[:, :HD]
                totals[head] = mixed[:, HD:]

        pipelined(heads, scores_of, use)

    for blocks in sizes:
        pl.when(jnp.int32(count) == blocks)(functools.partial(run, blocks))


def add_blocks(queries, keys, values, peaks, totals, sums):
    def scores_of(head):
        return rows_dot(queries[head], keys)

    def use(group, scores):
        old = [peaks[head] for head in group]
        tops = [jnp.maximum(peak, row_peak(score)) for peak, score in zip(old, scores)]
        for head, before, peak, mixed in zip(group, old, tops, weighted(scores, tops, values)):
            factor = jnp.exp2(before - peak)
            peaks[head] = peak
            sums[head] = sums[head] * factor + mixed[:, :HD]
            totals[head] = totals[head] * factor + mixed[:, HD:]

    pipelined(queries.shape[0], scores_of, use)


def continue_text(queries, kv_ref, arrive, begin, end, peaks, totals, sums):
    def step(chunk, carry):
        arrive(chunk)
        keys, values = load_blocks(kv_ref, chunk * CHUNK, CHUNK, queries.shape[1])
        add_blocks(queries, keys, values, peaks, totals, sums)
        return carry

    lax.fori_loop(begin, end, step, 0)


def pair_copies(source, held, sems):
    blocks = [pl.ds(start, PAIR) for start in range(0, source.shape[0], PAIR)]
    return [
        pltpu.make_async_copy(source.at[block], held.at[block], sems.at[turn]) for turn, block in enumerate(blocks)
    ]


def chunk_copy(source, held, sems, chunk):
    blocks = pl.ds(chunk * CHUNK, CHUNK)
    return pltpu.make_async_copy(source.at[blocks], held.at[blocks], sems.at[chunk])


def packed_logs(peaks, totals):
    heads, rows, _ = peaks.shape
    owner = lax.rem(lax.broadcasted_iota(jnp.int32, (rows, HD), 1), heads)
    peak, total = peaks[0], totals[0]
    for head in range(1, heads):
        peak = jnp.where(owner == head, peaks[head], peak)
        total = jnp.where(owner == head, totals[head], total)
    return peak + jnp.log2(total)


def first_kernel(
    q_ref,
    kv_ref,
    out_ref,
    logs_ref,
    ship_ref,
    kv_held,
    out_held,
    logs_held,
    ship_held,
    queries,
    peaks,
    totals,
    sums,
    q_sems,
    kv_sems,
    out_sems,
):
    heads, rows, _ = queries.shape
    slots = kv_ref.shape[0]
    late, index = plane_of(slots)
    count = slots - 1 - index
    masked = jnp.where(late == 1, index, jnp.maximum(count - 1, 0)) // CHUNK
    q_copies = pair_copies(q_ref, queries, q_sems)

    def chunk_of(chunk):
        return chunk_copy(kv_ref, kv_held, kv_sems, chunk)

    q_copies[0].start()
    chunk_of(masked).start()
    for q_copy in q_copies[1:]:
        q_copy.start()
    for chunk in range(slots // CHUNK):
        pl.when(chunk < masked)(chunk_of(chunk).start)

    sizes = range(1, CHUNK + 1)
    blocks = jnp.where(late == 1, CHUNK, jnp.maximum(count, 1) - masked * CHUNK)
    limit = jnp.where(late == 1, index * rows, count * rows - 1)
    beyond = jnp.where(late == 1, (index + 1) * rows, slots * rows)
    chunk_of(masked).wait()
    start_text(queries, q_copies, kv_held, masked, blocks, sizes, late, limit, beyond, peaks, totals, sums)
    continue_text(queries, kv_held, lambda chunk: chunk_of(chunk).wait(), 0, masked, peaks, totals, sums)
    logs = packed_logs(peaks, totals)

    @pl.when(late == 1)
    def _():
        logs_held[...] = logs
        logs_copy = pltpu.make_async_copy(logs_held, logs_ref, out_sems.at[0])
        logs_copy.start()
        for head in range(heads):
            out_held[:, head_columns(head)] = sums[head] / totals[head]
        out_copy = pltpu.make_async_copy(out_held, out_ref, out_sems.at[1])
        out_copy.start()
        logs_copy.wait()
        out_copy.wait()

    @pl.when(late == 0)
    def _():
        for head in range(heads):
            ship_held[:rows, head_columns(head)] = (sums[head] / totals[head]).astype(jnp.bfloat16)
        by_head = logs.T[:heads]
        high = by_head.astype(jnp.bfloat16).astype(jnp.float32)
        middle = (by_head - high).astype(jnp.bfloat16).astype(jnp.float32)
        low = by_head - high - middle
        ship_held[rows:, :rows] = jnp.concatenate([high, middle], axis=0).astype(jnp.bfloat16)
        ship_held[rows:, rows : 2 * rows] = jnp.concatenate([low, low], axis=0).astype(jnp.bfloat16)
        ship_held[rows:, 2 * rows :] = jnp.zeros_like(ship_held[rows:, 2 * rows :])
        ship_copy = pltpu.make_async_copy(ship_held, ship_ref, out_sems.at[2])
        ship_copy.start()
        ship_copy.wait()


def run_start(ids_ref, image):
    count = ids_ref.shape[0]
    start = jnp.int32(0)
    step = count // 2
    while step:
        start = jnp.where(ids_ref[start + step - 1] < image, start + step, start)
        step //= 2
    return start + (ids_ref[start] < image).astype(jnp.int32)


def second_kernel(
    q_ref,
    kv_ref,
    early_ref,
    early_logs_ref,
    extra_ref,
    att_ref,
    logs_ref,
    kv_held,
    early_held,
    early_logs_held,
    extra_held,
    queries,
    peaks,
    totals,
    sums,
    sems,
    q_sems,
    kv_sems,
):
    heads, rows, _ = queries.shape
    slots = kv_ref.shape[0]
    chunks = slots // CHUNK
    late, index = plane_of(slots)
    masked = index // CHUNK
    q_copies = pair_copies(q_ref, queries, q_sems)
    early_copy = pltpu.make_async_copy(early_ref, early_held, sems.at[0])
    logs_copy = pltpu.make_async_copy(early_logs_ref, early_logs_held, sems.at[1])
    extra_copy = pltpu.make_async_copy(extra_ref, extra_held.at[0], sems.at[2])

    def chunk_of(chunk):
        return chunk_copy(kv_ref, kv_held, kv_sems, chunk)

    def arrive(chunk):
        chunk_of(chunk).wait()

    q_copies[0].start()

    @pl.when(late == 0)
    def _():
        chunk_of(masked).start()
        for q_copy in q_copies[1:]:
            q_copy.start()
        for chunk in range(chunks):
            pl.when(chunk < masked)(chunk_of(chunk).start)

    @pl.when(late == 1)
    def _():
        logs_copy.start()
        early_copy.start()
        extra_copy.start()
        for q_copy in q_copies[1:]:
            q_copy.start()
        for chunk in range(chunks):
            pl.when(chunk > masked)(chunk_of(chunk).start)

    @pl.when(late == 0)
    def _():
        arrive(masked)
        start_text(queries, q_copies, kv_held, masked, CHUNK, (CHUNK,), 1, index * rows, slots * rows, peaks, totals, sums)

    @pl.when(late == 1)
    def _():
        logs_copy.wait()
        early_copy.wait()
        for head in range(heads):
            peaks[head] = jnp.broadcast_to(early_logs_held[:, head : head + 1], (rows, HD))
            totals[head] = jnp.ones_like(totals[head])
            sums[head] = early_held[:, head_columns(head)]
        for q_copy in q_copies:
            q_copy.wait()
        extra_copy.wait()
        add_blocks(queries, *load_blocks(extra_held, 0, 1, rows), peaks, totals, sums)

    begin = jnp.where(late == 1, masked + 1, 0)
    end = jnp.where(late == 1, chunks, masked)
    continue_text(queries, kv_held, arrive, begin, end, peaks, totals, sums)
    logs_ref[...] = packed_logs(peaks, totals)
    for head in range(heads):
        att_ref[:, head_columns(head)] = sums[head] / totals[head]


def cross_kernel(ids_ref, q_ref, gate_ref, kv_ref, cross_ref, kv_held, queries, q_sem, kv_sems):
    heads, rows, _ = queries.shape
    sources, images, part, _ = kv_ref.shape
    width = sources * part
    first = jnp.maximum(ids_ref[0], 0)
    last = ids_ref[rows - 1]
    q_copy = pltpu.make_async_copy(q_ref, queries, q_sem)

    def image_copy(offset):
        return pltpu.make_async_copy(kv_ref.at[:, offset], kv_held.at[offset], kv_sems.at[offset])

    q_copy.start()
    for offset in range(images):
        image_copy(offset).start()
    gates = jnp.tanh(gate_ref[...])
    cross_ref[...] = jnp.zeros_like(cross_ref)
    q_copy.wait()

    def attend(offset, carry):
        image_copy(offset).wait()
        keys = kv_held[offset, :, :, :HD].reshape(width, HD)
        values = kv_held[offset, :, :, HD:].reshape(width, HD)
        keys = jnp.concatenate([keys, keys], axis=1)
        values = jnp.concatenate([values, jnp.ones_like(values)], axis=1)
        row = lax.broadcasted_iota(jnp.int32, (rows, HD), 0)
        begin = run_start(ids_ref, first + offset)
        end = run_start(ids_ref, first + offset + 1)
        matches = jnp.logical_and(row >= begin, row < end)

        def scores_of(head):
            return rows_dot(queries[head], keys)

        def use(group, scores):
            tops = [row_peak(score) for score in scores]
            for head, mixed in zip(group, weighted(scores, tops, values)):
                gated = gates[head : head + 1] * (mixed[:, :HD] / mixed[:, HD:])
                columns = head_columns(head)
                cross_ref[:, columns] = jnp.where(matches, gated, cross_ref[:, columns])

        pipelined(heads, scores_of, use)
        return carry

    count = jnp.clip(last - first + 1, 0, images)
    lax.fori_loop(0, count, attend, 0)
    for offset in range(images):
        pl.when(offset >= count)(image_copy(offset).wait)


def final_kernel(slots, att_ref, logs_ref, cross_ref, sent_ref, coded_ref, down_ref, out_ref, rank_ref):
    rows, width = att_ref.shape
    heads = width // HD
    late, _ = plane_of(slots)

    @pl.when(late == 0)
    def _():
        out_ref[...] = (att_ref[...] + cross_ref[...]).astype(jnp.bfloat16)

    @pl.when(late == 1)
    def _():
        start = pl.multiple_of(pl.program_id(0) * rows, rows)
        upper = coded_ref[:, pl.ds(start, rows)].astype(jnp.float32)
        low = coded_ref[:, pl.ds(start + 2 * rows, rows)].astype(jnp.float32)
        by_head = upper[:heads] + upper[heads:] + low[:heads]
        sent_logs = jnp.concatenate([by_head] * (HD // heads), axis=0).T
        own_logs = logs_ref[...]
        peak = jnp.maximum(own_logs, sent_logs)
        own_part = jnp.exp2(own_logs - peak)
        sent_part = jnp.exp2(sent_logs - peak)
        whole = own_part + sent_part
        own_part = own_part / whole
        sent_part = sent_part / whole
        for head in range(heads):
            columns = head_columns(head)
            mixed = own_part[:, head : head + 1] * att_ref[:, columns]
            mixed = mixed + sent_part[:, head : head + 1] * sent_ref[:, columns].astype(jnp.float32)
            out_ref[:, columns] = (mixed + cross_ref[:, columns]).astype(jnp.bfloat16)

    rank_ref[...] = rows_dot(down_ref[...], out_ref[...]).astype(jnp.bfloat16)


def swap_cores(values):
    vis = lax.axis_size("vis")
    return lax.ppermute(values, "vis", [(v, v ^ 1) for v in range(vis)])


def turn_pairs(values, turn):
    vis = lax.axis_size("vis")
    return lax.ppermute(values, "vis", [(v, (v + 2 * turn) % vis) for v in range(vis)])


def local(
    text_q,
    text_k,
    text_v,
    cross_q,
    vision_k,
    vision_v,
    q_gain,
    k_gain,
    head_gate,
    adapter_down,
    image_ids,
    image_slot,
):
    rows, q_width = text_q.shape
    heads = q_width // HD
    ctx = lax.axis_size("ctx")
    vis = lax.axis_size("vis")
    half = ctx // 2
    part = vision_k.shape[1]
    small = pltpu.CompilerParams(vmem_limit_bytes=8 * 2**20)
    large = pltpu.CompilerParams(vmem_limit_bytes=58 * 2**20)
    shape = jax.ShapeDtypeStruct

    sent_q = lax.ppermute(text_q, "ctx", [(c, ctx - 1 - c) for c in range(half, ctx)])
    payload = pl.pallas_call(
        payload_kernel,
        out_shape=shape((rows, 2 * HD), jnp.bfloat16),
        in_specs=[VMEM, VMEM],
        out_specs=VMEM,
        compiler_params=small,
    )(text_k, text_v)
    other = lax.ppermute(payload, "ctx", [(c, c + half) for c in range(half)])
    outgoing = pl.pallas_call(
        slots_kernel,
        out_shape=shape((half, rows + ID_ROWS, 2 * HD), jnp.bfloat16),
        in_specs=[VMEM] * 3,
        out_specs=VMEM,
        compiler_params=small,
    )(payload, other, image_ids.reshape(-1, HD))
    outgoing, sent_q = lax.optimization_barrier((outgoing, sent_q))
    planes = [list(range(half)), list(range(half, ctx))]
    text_kv = lax.all_to_all(outgoing, "ctx", 0, 0, axis_index_groups=planes)

    split = shape((heads, rows, 2 * HD), jnp.bfloat16)
    gates = jnp.broadcast_to(head_gate[:, None], (heads, HD))
    first_split, second_split, cross_split = pl.pallas_call(
        functools.partial(prepare_kernel, half),
        out_shape=(split, split, split),
        in_specs=[VMEM] * 4,
        out_specs=(VMEM, VMEM, VMEM),
        compiler_params=pltpu.CompilerParams(vmem_limit_bytes=16 * 2**20),
    )(text_q, sent_q, cross_q, q_gain.reshape(1, HD))
    pairs = vis // 2
    kept, swapped = pl.pallas_call(
        vision_kernel,
        out_shape=[shape((pairs, part, 2 * HD), jnp.bfloat16)] * 2,
        in_specs=[VMEM] * 3,
        out_specs=[VMEM] * 2,
        compiler_params=small,
    )(vision_k[0], vision_v[0], k_gain.reshape(1, HD))
    down = adapter_down.T
    kept, swapped, down, gates, _ = lax.optimization_barrier((kept, swapped, down, gates, outgoing))
    both = jnp.stack([kept, swap_cores(swapped)], axis=1)
    slots_kv = jnp.stack([both[0]] + [turn_pairs(both[turn], turn) for turn in range(1, pairs)])
    other_kv = lax.ppermute(slots_kv, "ctx", [(c, (c + half) % ctx) for c in range(ctx)])

    firsts = text_kv[:, rows, 0].astype(jnp.int32)
    picked = pl.pallas_call(
        select_kernel,
        out_shape=shape((half, 2, 2 * part, 2 * HD), jnp.bfloat16),
        in_specs=[SMEM] * 2 + [VMEM] * 2,
        out_specs=VMEM,
        scratch_shapes=[pltpu.VMEM(image_slot.shape + (2 * part, 2 * HD), jnp.bfloat16)],
        compiler_params=small,
    )(firsts, image_slot, slots_kv, other_kv)
    image_kv = lax.all_to_all(picked, "ctx", 0, 0, axis_index_groups=planes)

    state = pltpu.VMEM((heads, rows, HD), jnp.float32)
    wide = shape((rows, q_width), jnp.float32)
    logs = shape((rows, HD), jnp.float32)
    cost = pl.CostEstimate(flops=9 * 10**9, bytes_accessed=6 * 10**6, transcendentals=9 * 10**6)
    buffers = [pltpu.VMEM(text_kv.shape, text_kv.dtype)]
    states = [pltpu.VMEM(split.shape, split.dtype), state, state, state]
    chunk_sems = pltpu.SemaphoreType.DMA((half // CHUNK,))
    pair_sems = pltpu.SemaphoreType.DMA((heads // PAIR,))
    early_att, early_logs, ship = pl.pallas_call(
        first_kernel,
        out_shape=(wide, logs, shape((rows + 2 * heads, q_width), jnp.bfloat16)),
        in_specs=[ANY] * 2,
        out_specs=(ANY, ANY, ANY),
        scratch_shapes=buffers
        + [
            pltpu.VMEM(wide.shape, wide.dtype),
            pltpu.VMEM(logs.shape, logs.dtype),
            pltpu.VMEM((rows + 2 * heads, q_width), jnp.bfloat16),
        ]
        + states
        + [pair_sems, chunk_sems, pltpu.SemaphoreType.DMA((3,))],
        compiler_params=large,
        cost_estimate=cost,
    )(first_split, text_kv)
    sent = lax.ppermute(ship, "ctx", [(c, ctx - 1 - c) for c in range(half)])
    att, att_logs = pl.pallas_call(
        second_kernel,
        out_shape=(wide, logs),
        in_specs=[ANY] * 5,
        out_specs=(VMEM, VMEM),
        scratch_shapes=buffers
        + [pltpu.VMEM(wide.shape, wide.dtype), pltpu.VMEM(logs.shape, logs.dtype), pltpu.VMEM((1,) + other.shape, other.dtype)]
        + states
        + [pltpu.SemaphoreType.DMA((3,)), pair_sems, chunk_sems],
        compiler_params=large,
        cost_estimate=cost,
    )(second_split, text_kv, early_att, early_logs, other)
    crossed = pl.pallas_call(
        cross_kernel,
        out_shape=wide,
        in_specs=[SMEM, ANY, VMEM, ANY],
        out_specs=VMEM,
        scratch_shapes=[
            pltpu.VMEM((2, half, 2 * part, 2 * HD), image_kv.dtype),
            states[0],
            pltpu.SemaphoreType.DMA,
            pltpu.SemaphoreType.DMA((2,)),
        ],
        compiler_params=pltpu.CompilerParams(vmem_limit_bytes=20 * 2**20),
        cost_estimate=cost,
    )(image_ids, cross_split, gates, image_kv)
    rank = adapter_down.shape[1]
    block = rows // 2

    def row_block(columns):
        return pl.BlockSpec((block, columns), lambda turn: (turn, 0))

    def whole(array_shape):
        return pl.BlockSpec(array_shape, lambda turn: (0, 0))

    mixed_out, partial = pl.pallas_call(
        functools.partial(final_kernel, half),
        grid=(2,),
        out_shape=(shape((rows, q_width), jnp.bfloat16), shape((rank, rows), jnp.bfloat16)),
        in_specs=[
            row_block(q_width),
            row_block(HD),
            row_block(q_width),
            row_block(q_width),
            pl.BlockSpec((2 * heads, q_width), lambda turn: (rows // (2 * heads), 0)),
            whole(down.shape),
        ],
        out_specs=(row_block(q_width), pl.BlockSpec((rank, block), lambda turn: (0, turn))),
        compiler_params=pltpu.CompilerParams(vmem_limit_bytes=12 * 2**20),
    )(att, att_logs, crossed, sent, sent, down)
    chip_sum = (partial.astype(jnp.float32) + swap_cores(partial).astype(jnp.float32)).astype(jnp.bfloat16)
    summed = chip_sum.astype(jnp.float32)
    for turn in range(1, pairs):
        summed = summed + turn_pairs(chip_sum, turn).astype(jnp.float32)
    lowrank = summed.T
    return (mixed_out, lowrank)


def solution(mesh):
    return jax.shard_map(
        local,
        mesh=mesh,
        in_specs=(
            P("ctx", "vis"),
            P("ctx", "vis"),
            P("ctx", "vis"),
            P("ctx", "vis"),
            P("vis", "ctx", None),
            P("vis", "ctx", None),
            P(),
            P(),
            P("vis"),
            P("vis", None),
            P("ctx"),
            P(),
        ),
        out_specs=(P("ctx", "vis"), P("ctx", None)),
        check_vma=False,
    )
```
